512 devices in a mesh: dp: 32 (over y, x, core), tm: 16 (over z).
Axes of the slice: x: 4, y: 4, z: 16, core: 2. Of those that a mesh axis runs over, the one named last changes fastest.
Arguments:
- phonemes: bfloat16 [32, 256, 1024], P('dp', 'tm'), may hold values from -6 to 6
- durations: int32 [32, 256], P('dp', 'tm'), may hold values from 1 to 32, 2048 in all within a row
- conv_weight: bfloat16 [9, 1024, 2048], P(None, None, 'tm'), may hold values from -0.0625 to 0.0625
- out_weight: bfloat16 [2048, 1024], P('tm', 'dp'), may hold values from -0.125 to 0.125
- norm_gain: float32 [1024], replicated, may hold values from 0.1 to 1.9
Outputs:
- decoded: bfloat16 [32, 2048, 1024], P('dp', 'tm')
The draws below stay inside these ranges and needn't reach their ends.
Inputs may be any that keep to these rules, and one draw needn't show every extreme that they name: Each utterance's durations sum to 2048, and in each utterance some phoneme lasts exactly 32 frames.
All inputs are finite; a program needn't handle non-finite values. No bound on the sum of `durations` on one device may be relied on, other than what follows from the above.
Results may differ from the reference program's by a relative error of at most 0.015.
Values may be sent and summed in bfloat16 or wider, within the bound.
A program may use at most 64 MiB of HBM per device.

```python
import math
import jax
import jax.numpy as jnp
import numpy as np
from jax import lax

D = 1024
HID = 2048
KER = 9
MAXDUR = 32
UTT = 32
FRAMES = 2048
PHONES = 256
HID_DEV = 128


def block_levels(own_key, dims, shards, low, top_value):
    def one(dim, shards_of):
        draws = jax.random.uniform(jax.random.fold_in(jax.random.fold_in(own_key, 6), dim), (shards_of,), jnp.float32, low / len(shards), top_value / len(shards))
        return jnp.repeat(jnp.exp(draws), dims[dim] // shards_of).reshape((-1,) + (1,) * (len(dims) - dim - 1))

    factor_of = one(*shards[0])
    for cut in shards[1:]:
        factor_of = factor_of * one(*cut)
    return factor_of


def length_profile(number_of, total, bound, slope):
    weights = [(1 << 20) // math.isqrt(grade ** slope) + 1 for grade in range(2, number_of + 1)]
    spare, given = total - bound - (number_of - 1), [1] * (number_of - 1)
    while spare > 0:
        free = [i for i in range(number_of - 1) if given[i] < bound]
        mass, budget = sum([weights[i] for i in free]), spare
        for i in free:
            more = min(bound - given[i], max(1, budget * weights[i] // mass), spare)
            given[i] = given[i] + more
            spare = spare - more
    return np.array([bound] + given)


def ragged(rng, count, total, most, slope):
    if count == 2:
        one = jax.random.randint(rng, (), max(1, total - most), min(most, total - 1) + 1)
        return jnp.stack([one, total - one])
    tallies = jnp.asarray(length_profile(count, total, most, slope), jnp.int32)
    pairs = (count - 1) // 2
    giver, receiver = tallies[1:1 + 2 * pairs:2], tallies[2:2 + 2 * pairs:2]
    slack = jnp.minimum(giver - 1, most - receiver)
    passed = jax.random.randint(jax.random.fold_in(rng, 1), (pairs,), 0, 1 << 20) % (slack + 1)
    tallies = tallies.at[1:1 + 2 * pairs:2].set(giver - passed).at[2:2 + 2 * pairs:2].set(receiver + passed)
    return tallies[jax.random.permutation(jax.random.fold_in(rng, 2), count)]


def bell_draw(own_key, extent, deviation, most, shards=(), kind=jnp.bfloat16):
    factor_of = block_levels(own_key, extent, shards, -0.22, 0.18) if shards else 1.0
    result = jax.random.normal(own_key, extent, jnp.float32) * deviation * factor_of
    return jnp.minimum(jnp.maximum(result, -most), most).astype(kind)


def setup_inputs(seed: int = 0) -> dict:
    streams_of = jax.random.split(jax.random.key(seed), 6)
    phonemes = bell_draw(streams_of[0], (UTT, PHONES, D), 1.0, 6.0, ((0, 32), (1, 16)))
    durations = jax.vmap(lambda own: ragged(own, PHONES, FRAMES, MAXDUR, 2))(jax.random.split(streams_of[1], UTT)).reshape((UTT, PHONES)).astype(jnp.int32)
    conv_weight = bell_draw(streams_of[2], (KER, D, HID), (KER * D) ** -0.5, 0.0625, ((2, 16),))
    out_weight = bell_draw(streams_of[3], (HID, D), HID ** -0.5, 0.125, ((0, 16), (1, 32)))
    norm_gain = jnp.clip(1.0 + 0.18 * jax.random.normal(streams_of[4], (D,), jnp.float32), 0.1, 1.9)
    return dict(phonemes=phonemes, durations=durations, conv_weight=conv_weight, out_weight=out_weight, norm_gain=norm_gain)


def reference(phonemes, durations, conv_weight, out_weight, norm_gain):
    margin = KER // 2
    groups = HID // HID_DEV

    def utterance(pieces):
        phone_rows, phone_lengths = pieces
        phone_ends = jnp.cumsum(phone_lengths).astype(jnp.int32)
        positions = jnp.arange(FRAMES, dtype=jnp.int32)
        owner_phone = jnp.searchsorted(phone_ends, positions, side='right').astype(jnp.int32)
        frames = phone_rows[owner_phone]
        padded = jnp.pad(frames, ((margin, margin), (0, 0)))
        pre_act = jnp.zeros((FRAMES, HID), jnp.float32)
        for offset in range(KER):
            pre_act = pre_act + jnp.dot(padded[offset:offset + FRAMES], conv_weight[offset], preferred_element_type=jnp.float32)
        hidden = jnp.maximum(pre_act, 0.0).astype(jnp.bfloat16)

        def add_group(group_index, running):
            first_unit = (group_index * HID_DEV).astype(jnp.int32)
            hidden_block = lax.dynamic_slice_in_dim(hidden, first_unit, HID_DEV, 1)
            weights = lax.dynamic_slice_in_dim(out_weight, first_unit, HID_DEV, 0)
            rounded = jnp.dot(hidden_block, weights, preferred_element_type=jnp.float32).astype(jnp.bfloat16)
            rounded = lax.optimization_barrier(rounded)
            return running + rounded.astype(jnp.float32)
        summed = lax.fori_loop(0, groups, add_group, frames.astype(jnp.float32))
        average = lax.optimization_barrier(jnp.mean(summed, axis=-1, keepdims=True))
        centered = summed - average
        spread = lax.optimization_barrier(jnp.mean(centered * centered, axis=-1, keepdims=True))
        decoded = centered * lax.rsqrt(spread + 1e-05) * norm_gain.astype(jnp.float32)
        return decoded.astype(jnp.bfloat16)
    return lax.map(utterance, (phonemes, durations))
```

```python
import jax
import jax.numpy as jnp
from jax import lax
from jax.experimental import pallas as pl
from jax.experimental.pallas import tpu as pltpu
from jax.sharding import PartitionSpec as P

MESH = pl.DeviceIdType.MESH
BF, F32 = jnp.bfloat16, jnp.float32
NZ = 16
NEAR = (0, 1, 15, 2)
TAPS = 9
HALO = TAPS // 2
ROWS = 144


def chunk_of(offset):
    for j in range(4):
        for r in range(4):
            if (NEAR[j] + 4 * r) % NZ == offset:
                return j, r


def kernel(phon_in, dur_in, conv_w, out_w, gain, out,
           phon, dur_own, dur_all, w, zc, w2, hid_out, hid_in, acc,
           w_sem, ps, pr, ds, dr, ws, wr, xs, xr, cs, cr, hs, hr):
    z = lax.axis_index("tm")
    dp = lax.axis_index("dp")
    y, x, c = dp // 8, lax.rem(dp // 2, 4), lax.rem(dp, 2)

    def zpeer(o):
        return (dp, lax.rem(z + o, NZ))

    def xpeer(d):
        return (y * 8 + lax.rem(x + d, 4) * 2 + c, z)

    def ypeer(d):
        return (lax.rem(y + d, 4) * 8 + x * 2 + c, z)

    sibling = (y * 8 + x * 2 + 1 - c, z)

    def remote(src, dst, ssem, rsem, dev):
        return pltpu.make_async_remote_copy(
            src_ref=src, dst_ref=dst, send_sem=ssem, recv_sem=rsem, device_id=dev, device_id_type=MESH)

    barrier = pltpu.get_barrier_semaphore()
    peers = [zpeer(o) for o in range(1, NZ)] + [xpeer(d) for d in (1, 2, 3)] + [ypeer(d) for d in (1, 2, 3)] + [sibling]
    for dev in peers:
        pl.semaphore_signal(barrier, inc=1, device_id=dev, device_id_type=MESH)

    w_copy = pltpu.make_async_copy(conv_w, w, w_sem)
    w_copy.start()

    phon[0, 0] = phon_in[0]
    dur_own[...] = jnp.zeros_like(dur_own)
    dur_own[:, 0:16] = dur_in[...]
    dur_all[0] = dur_own[...]
    eye = (lax.broadcasted_iota(jnp.int32, (32, 32), 0) == lax.broadcasted_iota(jnp.int32, (32, 32), 1))
    w2_own = lax.dot_general(eye.astype(F32).astype(BF), out_w[...], (((1,), (1,)), ((), ())),
                             preferred_element_type=F32).astype(BF)
    w2[y, x, c, 0, :, 0:128] = w2_own[0:16]
    w2[y, x, c, 1, :, 0:128] = w2_own[16:32]

    def far(r):
        return (remote(phon.at[0, 0], phon.at[0, r], ps.at[r], pr.at[r], zpeer(4 * r)),
                remote(w2.at[y, x, c, :, :, pl.ds(0, 128)], w2.at[y, x, c, :, :, pl.ds(128 * r, 128)],
                       ws.at[r], wr.at[r], zpeer(4 * r)))

    def near(j, r):
        i = 4 * j + r
        return (remote(phon.at[0, r], phon.at[j, r], ps.at[i], pr.at[i], zpeer(NEAR[j])),
                remote(w2.at[y, x, c, :, :, pl.ds(128 * r, 128)], w2.at[y, x, c, :, :, pl.ds(128 * i, 128)],
                       ws.at[i], wr.at[i], zpeer(NEAR[j])))

    def dur_copy(o):
        return remote(dur_own, dur_all.at[o], ds.at[o], dr.at[o], zpeer(o))

    pl.semaphore_wait(barrier, len(peers))

    fars = {r: far(r) for r in (2, 1, 3)}
    nears = {(j, r): near(j, r) for j in (1, 2, 3) for r in range(4)}
    durs = [dur_copy(o) for o in range(1, NZ)]
    for r in (2, 1, 3):
        fars[r][0].start()
    for j in (3, 1, 2):
        nears[j, 0][0].start()
    for d in durs:
        d.start()
    for r in (2, 1, 3):
        fars[r][1].start()
    for j in (3, 1, 2):
        nears[j, 0][1].start()
    for r in (1, 3, 2):
        fars[r][0].wait_recv()
        for j in (3, 1, 2):
            nears[j, r][0].start()
    for r in (1, 3, 2):
        fars[r][1].wait_recv()
        for j in (3, 1, 2):
            nears[j, r][1].start()

    def products(j):
        rows = phon[j].reshape(64, 1024)
        for k in range(0, TAPS, 2):
            taps = [w[t] for t in range(k, min(k + 2, TAPS))]
            cols = jnp.concatenate(taps, axis=1) if len(taps) > 1 else taps[0]
            prod = jnp.dot(rows, cols, preferred_element_type=F32)
            high = prod.astype(BF)
            low = (prod - high.astype(F32)).astype(BF)
            width = 128 * len(taps)
            zc[64 * j:64 * j + 64, 128 * k:128 * k + width] = high
            zc[256 + 64 * j:256 + 64 * j + 64, 128 * k:128 * k + width] = low

    w_copy.wait()
    products(0)

    for d in durs:
        d.wait_recv()
    lengths = jnp.concatenate([dur_all[o] for o in range(NZ)], axis=0).astype(F32).astype(BF)
    col = lax.broadcasted_iota(jnp.int32, (1, 256), 1)
    near_slot, far_slot, place = col // 64, lax.rem(col // 16, 4), lax.rem(col, 16)
    near_off = jnp.where(near_slot == 0, 0, jnp.where(near_slot == 1, 1, jnp.where(near_slot == 2, 15, 2)))
    col_off = lax.rem(near_off + 4 * far_slot, NZ)
    col_chunk = lax.rem(z + NZ - col_off, NZ)
    row_chunk = lax.rem(z + NZ - lax.broadcasted_iota(jnp.int32, (NZ, 256), 0), NZ)
    lane = lax.broadcasted_iota(jnp.int32, (128, 256), 0)
    upto = ((lane <= place) & (lane < 16)).astype(F32).astype(BF)
    exact = (lane == place).astype(F32).astype(BF)
    whole = (lane < 16).astype(F32).astype(BF)
    within = jnp.dot(lengths, upto, preferred_element_type=F32)
    single = jnp.dot(lengths, exact, preferred_element_type=F32)
    total = jnp.dot(lengths, whole, preferred_element_type=F32)
    same = row_chunk == col_chunk
    ends = jnp.sum(jnp.where(same, within, jnp.where(row_chunk < col_chunk, total, 0.0)), axis=0, keepdims=True)
    sizes = jnp.sum(jnp.where(same, single, 0.0), axis=0, keepdims=True)
    starts = ends - sizes

    def one_hot(first, count):
        frame = (lax.broadcasted_iota(jnp.int32, (count, 256), 0) + first).astype(F32)
        return jnp.where((frame >= starts) & (frame < ends), 1.0, 0.0).astype(BF)

    for j in (1, 2, 3):
        for r in range(4):
            nears[j, r][0].wait_recv()
        products(j)

    def hidden(o):
        block = lax.rem(z + o, NZ)
        pick = one_hot(block * 128 - HALO, ROWS)
        pick = jnp.concatenate([pick, pick], axis=1)
        total = jnp.zeros((128, 128), F32)
        for k in range(0, TAPS, 2):
            width = 128 * min(2, TAPS - k)
            got = jnp.dot(pick, zc[:, 128 * k:128 * k + width], preferred_element_type=F32)
            total = total + got[k:k + 128, 0:128]
            if width > 128:
                total = total + got[k + 1:k + 129, 128:256]
        return jnp.maximum(total, 0.0).astype(BF)

    def hid_copy(o):
        return remote(hid_out.at[o], hid_in.at[o], hs.at[o], hr.at[o], zpeer(o))

    def send_hidden(i, carry):
        o = lax.rem(8 + 7 * i, NZ)
        hid_out[o] = hidden(o)
        hid_copy(o).start()
        return carry

    lax.fori_loop(0, 4, send_hidden, 0)

    for j in (1, 2, 3):
        for r in range(4):
            nears[j, r][1].wait_recv()
    first = ([remote(w2.at[y, x, c, 0], w2.at[y, x, c, 0], xs.at[d], xr.at[d], xpeer(d)) for d in (1, 2, 3)]
             + [remote(w2.at[y, x, c, 1], w2.at[y, x, c, 1], xs.at[3 + d], xr.at[3 + d], ypeer(d)) for d in (1, 2, 3)])
    for i in (0, 2, 1, 3, 5, 4):
        first[i].start()

    lax.fori_loop(4, 8, send_hidden, 0)

    for d in first:
        d.wait_recv()
    second = ([remote(w2.at[y, :, c, 0], w2.at[y, :, c, 0], xs.at[6 + d], xr.at[6 + d], ypeer(d)) for d in (1, 2, 3)]
              + [remote(w2.at[:, x, c, 1], w2.at[:, x, c, 1], xs.at[9 + d], xr.at[9 + d], xpeer(d)) for d in (1, 2, 3)])
    for i in (0, 2, 1, 3, 5, 4):
        second[i].start()

    def to_sibling(i):
        if i < 4:
            part = w2.at[lax.rem(y + 4 - i, 4), :, c, 0]
        else:
            part = w2.at[:, lax.rem(x + 8 - i, 4), c, 1]
        return remote(part, part, cs.at[i], cr.at[i], sibling)

    cross = [to_sibling(i) for i in range(8)]
    cross[0].start()
    cross[4].start()

    lax.fori_loop(9, NZ, send_hidden, 0)
    hid_in[0] = hidden(0)

    acc[...] = jnp.dot(one_hot(z * 128, 128), phon[...].reshape(256, 1024), preferred_element_type=F32)

    for i in (1, 3, 2):
        second[i - 1].wait_recv()
        cross[i].start()
        second[2 + i].wait_recv()
        cross[4 + i].start()
    for d in cross:
        d.wait_recv()

    order = [(8 + 7 * i) % NZ for i in range(NZ)]
    groups = (order[0:4], order[4:8], [0] + order[9:12], order[12:16])
    for group in groups:
        for o in group:
            if o:
                hid_copy(o).wait_recv()
        left = jnp.concatenate([hid_in[o] for o in group], axis=1)
        slots = [chunk_of(o) for o in group]
        right = jnp.concatenate(
            [w2[:, :, :, :, :, 128 * (4 * j + r):128 * (4 * j + r) + 128].reshape(1024, 128) for j, r in slots], axis=1)
        acc[...] += lax.dot_general(left, right, (((1,), (1,)), ((), ())), preferred_element_type=F32)

    def norm(i, carry):
        rows = pl.ds(pl.multiple_of(i * 16, 16), 16)
        summed = acc[rows, :]
        centered = summed - jnp.mean(summed, axis=-1, keepdims=True)
        spread = jnp.mean(centered * centered, axis=-1, keepdims=True)
        out[0, rows, :] = (centered * lax.rsqrt(spread + 1e-5) * gain[...]).astype(BF)
        return carry

    lax.fori_loop(0, 8, norm, 0)

    for r in (1, 2, 3):
        for d in fars[r]:
            d.wait_send()
    for j in (1, 2, 3):
        for r in range(4):
            for d in nears[j, r]:
                d.wait_send()
    for d in durs + first + second + cross:
        d.wait_send()
    for o in range(1, NZ):
        hid_copy(o).wait_send()


def on_device(phonemes, durations, conv_weight, out_weight, norm_gain):
    vmem = pl.BlockSpec(memory_space=pltpu.VMEM)
    sems = pltpu.SemaphoreType.DMA
    return pl.pallas_call(
        kernel,
        out_shape=jax.ShapeDtypeStruct((1, 128, 1024), BF),
        in_specs=[vmem, vmem, pl.BlockSpec(memory_space=pl.ANY), vmem, vmem],
        out_specs=vmem,
        scratch_shapes=[
            pltpu.VMEM((4, 4, 16, 1024), BF),
            pltpu.VMEM((1, 128), jnp.int32),
            pltpu.VMEM((NZ, 1, 128), jnp.int32),
            pltpu.VMEM((TAPS, 1024, 128), BF),
            pltpu.VMEM((512, TAPS * 128), BF),
            pltpu.VMEM((4, 4, 2, 2, 16, 2048), BF),
            pltpu.VMEM((NZ, 128, 128), BF),
            pltpu.VMEM((NZ, 128, 128), BF),
            pltpu.VMEM((128, 1024), F32),
            sems, sems((16,)), sems((16,)), sems((16,)), sems((16,)), sems((16,)), sems((16,)),
            sems((13,)), sems((13,)), sems((8,)), sems((8,)), sems((16,)), sems((16,)),
        ],
        compiler_params=pltpu.CompilerParams(
            collective_id=0, has_side_effects=True, vmem_limit_bytes=48 * 1024 * 1024),
        cost_estimate=pl.CostEstimate(flops=4_000_000_000, bytes_accessed=4_000_000, transcendentals=0),
    )(phonemes, durations, conv_weight, out_weight, norm_gain.reshape(1, 1024))


def solution(mesh):
    placed = (P("dp", "tm", None), P("dp", "tm"), P(None, None, "tm"), P("tm", "dp"), P())
    return jax.shard_map(
        on_device, mesh=mesh, in_specs=placed, out_specs=P("dp", "tm", None), check_vma=False
    )
```

```python
import jax
import jax.numpy as jnp
from jax import lax
from jax.experimental import pallas as pl
from jax.experimental.pallas import tpu as pltpu
from jax.sharding import PartitionSpec as P

MESH = pl.DeviceIdType.MESH
BF, F32 = jnp.bfloat16, jnp.float32
NZ = 16
ORDER = (0, 1, 15, 2, 14, 5, 11, 3, 13, 4, 12, 6, 10, 7, 9, 8)
DIRECT = (5, 11, 2, 14, 1, 15)
ONWARD = {5: ((3, 8), (2, 7), (1, 6), (15, 4)), 11: ((13, 8), (14, 9), (15, 10), (1, 12)), 2: ((1, 3),), 14: ((15, 13),)}
TAPS = 9
HALO = TAPS // 2
ROWS = 144


def kernel(phon_in, dur_in, conv_w, out_w, gain_in, out,
           phon, dur_row, dur_own, dur_all, w, w2_own, gain, zc, w2, hid_out, hid_in, acc,
           in_sem, ps, pr, ds, dr, ws, wr, xs, xr, cs, cr, hs, hr):
    z = lax.axis_index("tm")
    dp = lax.axis_index("dp")
    y, x, c = dp // 8, lax.rem(dp // 2, 4), lax.rem(dp, 2)

    def zpeer(o):
        return (dp, lax.rem(z + o, NZ))

    def xpeer(d):
        return (y * 8 + lax.rem(x + d, 4) * 2 + c, z)

    def ypeer(d):
        return (lax.rem(y + d, 4) * 8 + x * 2 + c, z)

    sibling = (y * 8 + x * 2 + 1 - c, z)

    def remote(src, dst, ssem, rsem, dev):
        return pltpu.make_async_remote_copy(
            src_ref=src, dst_ref=dst, send_sem=ssem, recv_sem=rsem, device_id=dev, device_id_type=MESH)

    barrier = pltpu.get_barrier_semaphore()
    peers = [zpeer(o) for o in range(1, NZ)] + [xpeer(d) for d in (1, 2, 3)] + [ypeer(d) for d in (1, 2, 3)] + [sibling]
    for dev in peers:
        pl.semaphore_signal(barrier, inc=1, device_id=dev, device_id_type=MESH)

    phon_copy = pltpu.make_async_copy(phon_in.at[0], phon.at[0], in_sem.at[0])
    dur_load = pltpu.make_async_copy(dur_in, dur_row, in_sem.at[1])
    w2_copy = pltpu.make_async_copy(out_w, w2_own, in_sem.at[2])
    gain_copy = pltpu.make_async_copy(gain_in, gain, in_sem.at[3])
    w_copy = pltpu.make_async_copy(conv_w, w, in_sem.at[4])
    for d in (phon_copy, dur_load, w2_copy, gain_copy, w_copy):
        d.start()

    dur_own[...] = jnp.zeros_like(dur_own)
    dur_load.wait()
    dur_own[:, 0:16] = dur_row[...]
    dur_all[0] = dur_own[...]
    w2_copy.wait()
    w2[y, x, c, 0, :, 0:128] = w2_own[0:16]
    w2[y, x, c, 1, :, 0:128] = w2_own[16:32]
    phon_copy.wait()

    def phon_part(o, part):
        if part is None:
            return phon.at[ORDER.index(o)]
        return phon.at[ORDER.index(o), :, pl.ds(512 * part, 512)]

    def w2_part(o, part):
        lanes = pl.ds(128 * ORDER.index(o), 128)
        if part is None:
            return w2.at[y, x, c, :, :, lanes]
        return w2.at[y, x, c, part, :, lanes]

    def gather(place, ssem, rsem):
        def copy(held, to, there):
            part = None if there != 8 else (0 if held == 5 else 1)
            i = 0 if part == 1 else there
            return remote(place(held, part), place(there, part), ssem.at[i], rsem.at[i], zpeer(to))

        direct = {o: copy(0, o, o) for o in DIRECT}
        onward = {held: [copy(held, to, there) for to, there in jobs] for held, jobs in ONWARD.items()}
        return direct, onward

    def dur_copy(o):
        return remote(dur_own, dur_all.at[o], ds.at[o], dr.at[o], zpeer(o))

    pl.semaphore_wait(barrier, len(peers))

    rows_direct, rows_onward = gather(phon_part, ps, pr)
    cols_direct, cols_onward = gather(w2_part, ws, wr)
    durs = [dur_copy(o) for o in range(1, NZ)]
    for o in DIRECT:
        rows_direct[o].start()
    for d in durs:
        d.start()
    for o in (5, 11):
        rows_direct[o].wait_recv()
        for d in rows_onward[o]:
            d.start()
    for o in DIRECT:
        cols_direct[o].start()
    for o in (2, 14):
        rows_direct[o].wait_recv()
        for d in rows_onward[o]:
            d.start()
    for o in (5, 11, 2, 14):
        cols_direct[o].wait_recv()
        for d in cols_onward[o]:
            d.start()
    rows_onward = sum(rows_onward.values(), [])
    cols_onward = sum(cols_onward.values(), [])

    def products(j):
        rows = phon[4 * j:4 * j + 4].reshape(64, 1024)
        for k in range(0, TAPS, 2):
            taps = [w[t] for t in range(k, min(k + 2, TAPS))]
            cols = jnp.concatenate(taps, axis=1) if len(taps) > 1 else taps[0]
            prod = jnp.dot(rows, cols, preferred_element_type=F32)
            high = prod.astype(BF)
            low = (prod - high.astype(F32)).astype(BF)
            width = 128 * len(taps)
            zc[64 * j:64 * j + 64, 128 * k:128 * k + width] = high
            zc[256 + 64 * j:256 + 64 * j + 64, 128 * k:128 * k + width] = low

    w_copy.wait()
    for o in (1, 15):
        rows_direct[o].wait_recv()
    products(0)

    for d in durs:
        d.wait_recv()
    lengths = jnp.concatenate([dur_all[o] for o in range(NZ)], axis=0).astype(F32).astype(BF)
    col = lax.broadcasted_iota(jnp.int32, (1, 256), 1)
    slot, place = col // 16, lax.rem(col, 16)
    col_off = jnp.zeros_like(col)
    for i, o in enumerate(ORDER):
        col_off = jnp.where(slot == i, o, col_off)
    col_chunk = lax.rem(z + NZ - col_off, NZ)
    row_chunk = lax.rem(z + NZ - lax.broadcasted_iota(jnp.int32, (NZ, 256), 0), NZ)
    lane = lax.broadcasted_iota(jnp.int32, (128, 256), 0)
    upto = ((lane <= place) & (lane < 16)).astype(F32).astype(BF)
    exact = (lane == place).astype(F32).astype(BF)
    whole = (lane < 16).astype(F32).astype(BF)
    within = jnp.dot(lengths, upto, preferred_element_type=F32)
    single = jnp.dot(lengths, exact, preferred_element_type=F32)
    total = jnp.dot(lengths, whole, preferred_element_type=F32)
    same = row_chunk == col_chunk
    ends = jnp.sum(jnp.where(same, within, jnp.where(row_chunk < col_chunk, total, 0.0)), axis=0, keepdims=True)
    sizes = jnp.sum(jnp.where(same, single, 0.0), axis=0, keepdims=True)
    starts = ends - sizes

    def one_hot(first, count):
        frame = (lax.broadcasted_iota(jnp.int32, (count, 256), 0) + first).astype(F32)
        return jnp.where((frame >= starts) & (frame < ends), 1.0, 0.0).astype(BF)

    for d in rows_onward:
        d.wait_recv()
    for j in (1, 2, 3):
        products(j)

    def hidden(o):
        block = lax.rem(z + o, NZ)
        pick = one_hot(block * 128 - HALO, ROWS)
        pick = jnp.concatenate([pick, pick], axis=1)
        total = jnp.zeros((128, 128), F32)
        for k in range(0, TAPS, 2):
            width = 128 * min(2, TAPS - k)
            got = jnp.dot(pick, zc[:, 128 * k:128 * k + width], preferred_element_type=F32)
            total = total + got[k:k + 128, 0:128]
            if width > 128:
                total = total + got[k + 1:k + 129, 128:256]
        return jnp.maximum(total, 0.0).astype(BF)

    def hid_copy(o):
        return remote(hid_out.at[o], hid_in.at[o], hs.at[o], hr.at[o], zpeer(o))

    def send_hidden(i, carry):
        o = lax.rem(8 + 7 * i, NZ)
        hid_out[o] = hidden(o)
        hid_copy(o).start()
        return carry

    lax.fori_loop(0, 4, send_hidden, 0)

    for o in (1, 15):
        cols_direct[o].wait_recv()
    for d in cols_onward:
        d.wait_recv()
    first = ([remote(w2.at[y, x, c, 0], w2.at[y, x, c, 0], xs.at[d], xr.at[d], xpeer(d)) for d in (1, 2, 3)]
             + [remote(w2.at[y, x, c, 1], w2.at[y, x, c, 1], xs.at[3 + d], xr.at[3 + d], ypeer(d)) for d in (1, 2, 3)])
    for i in (0, 2, 1, 3, 5, 4):
        first[i].start()

    lax.fori_loop(4, 8, send_hidden, 0)

    for d in first:
        d.wait_recv()
    second = ([remote(w2.at[y, :, c, 0], w2.at[y, :, c, 0], xs.at[6 + d], xr.at[6 + d], ypeer(d)) for d in (1, 2, 3)]
              + [remote(w2.at[:, x, c, 1], w2.at[:, x, c, 1], xs.at[9 + d], xr.at[9 + d], xpeer(d)) for d in (1, 2, 3)])
    for i in (0, 2, 1, 3, 5, 4):
        second[i].start()

    def to_sibling(i):
        if i < 4:
            part = w2.at[lax.rem(y + 4 - i, 4), :, c, 0]
        else:
            part = w2.at[:, lax.rem(x + 8 - i, 4), c, 1]
        return remote(part, part, cs.at[i], cr.at[i], sibling)

    cross = [to_sibling(i) for i in range(8)]
    cross[0].start()
    cross[4].start()

    lax.fori_loop(9, NZ, send_hidden, 0)
    hid_in[0] = hidden(0)

    acc[...] = jnp.dot(one_hot(z * 128, 128), phon[...].reshape(256, 1024), preferred_element_type=F32)

    for i in (1, 3, 2):
        second[i - 1].wait_recv()
        cross[i].start()
        second[2 + i].wait_recv()
        cross[4 + i].start()
    for d in cross:
        d.wait_recv()

    order = [(8 + 7 * i) % NZ for i in range(NZ)]
    groups = (order[0:4], order[4:8], [0] + order[9:12], order[12:16])
    for group in groups:
        for o in group:
            if o:
                hid_copy(o).wait_recv()
        left = jnp.concatenate([hid_in[o] for o in group], axis=1)
        slots = [ORDER.index(o) for o in group]
        right = jnp.concatenate(
            [w2[:, :, :, :, :, 128 * i:128 * i + 128].reshape(1024, 128) for i in slots], axis=1)
        acc[...] += lax.dot_general(left, right, (((1,), (1,)), ((), ())), preferred_element_type=F32)

    gain_copy.wait()

    def norm(i, carry):
        rows = pl.ds(pl.multiple_of(i * 16, 16), 16)
        summed = acc[rows, :]
        centered = summed - jnp.mean(summed, axis=-1, keepdims=True)
        spread = jnp.mean(centered * centered, axis=-1, keepdims=True)
        out[0, rows, :] = (centered * lax.rsqrt(spread + 1e-5) * gain[...]).astype(BF)
        return carry

    lax.fori_loop(0, 8, norm, 0)

    for o in DIRECT:
        rows_direct[o].wait_send()
        cols_direct[o].wait_send()
    for d in rows_onward + cols_onward:
        d.wait_send()
    for d in durs + first + second + cross:
        d.wait_send()
    for o in range(1, NZ):
        hid_copy(o).wait_send()


def on_device(phonemes, durations, conv_weight, out_weight, norm_gain):
    vmem = pl.BlockSpec(memory_space=pltpu.VMEM)
    sems = pltpu.SemaphoreType.DMA
    return pl.pallas_call(
        kernel,
        out_shape=jax.ShapeDtypeStruct((1, 128, 1024), BF),
        in_specs=[pl.BlockSpec(memory_space=pltpu.HBM)] * 5,
        out_specs=vmem,
        scratch_shapes=[
            pltpu.VMEM((NZ, 16, 1024), BF),
            pltpu.VMEM((1, 16), jnp.int32),
            pltpu.VMEM((1, 128), jnp.int32),
            pltpu.VMEM((NZ, 1, 128), jnp.int32),
            pltpu.VMEM((TAPS, 1024, 128), BF),
            pltpu.VMEM((32, 128), BF),
            pltpu.VMEM((1, 1024), F32),
            pltpu.VMEM((512, TAPS * 128), BF),
            pltpu.VMEM((4, 4, 2, 2, 16, 2048), BF),
            pltpu.VMEM((NZ, 128, 128), BF),
            pltpu.VMEM((NZ, 128, 128), BF),
            pltpu.VMEM((128, 1024), F32),
            sems((5,)), sems((16,)), sems((16,)), sems((16,)), sems((16,)), sems((16,)), sems((16,)),
            sems((13,)), sems((13,)), sems((8,)), sems((8,)), sems((16,)), sems((16,)),
        ],
        compiler_params=pltpu.CompilerParams(
            collective_id=0, has_side_effects=True, vmem_limit_bytes=63 * 1024 * 1024),
        cost_estimate=pl.CostEstimate(flops=4_000_000_000, bytes_accessed=4_000_000, transcendentals=0),
    )(phonemes, durations, conv_weight, out_weight.T, norm_gain.reshape(1, 1024))


def solution(mesh):
    placed = (P("dp", "tm", None), P("dp", "tm"), P(None, None, "tm"), P("tm", "dp"), P())
    return jax.shard_map(
        on_device, mesh=mesh, in_specs=placed, out_specs=P("dp", "tm", None), check_vma=False
    )
```

```python
import jax
import jax.numpy as jnp
from jax import lax
from jax.experimental import pallas as pl
from jax.experimental.pallas import tpu as pltpu
from jax.sharding import PartitionSpec as P

MESH = pl.DeviceIdType.MESH
BF, F32 = jnp.bfloat16, jnp.float32
NZ = 16
ORDER = (0, 1, 15, 2, 14, 5, 11, 3, 13, 4, 12, 6, 10, 7, 9, 8)
DIRECT = (5, 11, 2, 14, 1, 15)
ONWARD = {5: ((3, 8), (2, 7), (1, 6), (15, 4)), 11: ((13, 8), (14, 9), (15, 10), (1, 12)), 2: ((1, 3),), 14: ((15, 13),)}
TAPS = 9
HALO = TAPS // 2
ROWS = 144


def kernel(phon_in, dur_in, conv_w, out_w, gain_in, out,
           phon, dur_row, dur_own, dur_all, w, w2_own, gain, zc, w2, hid_out, hid_in, acc,
           in_sem, ps, pr, ds, dr, ws, wr, xs, xr, cs, cr, hs, hr):
    z = lax.axis_index("tm")
    dp = lax.axis_index("dp")
    y, x, c = dp // 8, lax.rem(dp // 2, 4), lax.rem(dp, 2)

    def zpeer(o):
        return (dp, lax.rem(z + o, NZ))

    def xpeer(d):
        return (y * 8 + lax.rem(x + d, 4) * 2 + c, z)

    def ypeer(d):
        return (lax.rem(y + d, 4) * 8 + x * 2 + c, z)

    sibling = (y * 8 + x * 2 + 1 - c, z)

    def remote(src, dst, ssem, rsem, dev):
        return pltpu.make_async_remote_copy(
            src_ref=src, dst_ref=dst, send_sem=ssem, recv_sem=rsem, device_id=dev, device_id_type=MESH)

    barrier = pltpu.get_barrier_semaphore()
    peers = [zpeer(o) for o in range(1, NZ)] + [xpeer(d) for d in (1, 2, 3)] + [ypeer(d) for d in (1, 2, 3)] + [sibling]
    for dev in peers:
        pl.semaphore_signal(barrier, inc=1, device_id=dev, device_id_type=MESH)

    phon_copy = pltpu.make_async_copy(phon_in.at[0], phon.at[0], in_sem.at[0])
    dur_load = pltpu.make_async_copy(dur_in, dur_row, in_sem.at[1])
    w2_copy = pltpu.make_async_copy(out_w, w2_own, in_sem.at[2])
    gain_copy = pltpu.make_async_copy(gain_in, gain, in_sem.at[3])
    w_copy = pltpu.make_async_copy(conv_w, w, in_sem.at[4])
    for d in (phon_copy, dur_load, w2_copy, gain_copy, w_copy):
        d.start()

    dur_own[...] = jnp.zeros_like(dur_own)
    dur_load.wait()
    dur_own[:, 0:16] = dur_row[...]
    dur_all[0] = dur_own[...]
    w2_copy.wait()
    w2[y, x, c, 0, :, 0:128] = w2_own[0:16]
    w2[y, x, c, 1, :, 0:128] = w2_own[16:32]
    phon_copy.wait()

    def phon_part(o, part):
        if part is None:
            return phon.at[ORDER.index(o)]
        return phon.at[ORDER.index(o), :, pl.ds(512 * part, 512)]

    def w2_part(o, part):
        lanes = pl.ds(128 * ORDER.index(o), 128)
        if part is None:
            return w2.at[y, x, c, :, :, lanes]
        return w2.at[y, x, c, part, :, lanes]

    def gather(place, ssem, rsem):
        def copy(held, to, there):
            part = None if there != 8 else (0 if held == 5 else 1)
            i = 0 if part == 1 else there
            return remote(place(held, part), place(there, part), ssem.at[i], rsem.at[i], zpeer(to))

        direct = {o: copy(0, o, o) for o in DIRECT}
        onward = {held: [copy(held, to, there) for to, there in jobs] for held, jobs in ONWARD.items()}
        return direct, onward

    def dur_copy(o):
        return remote(dur_own, dur_all.at[o], ds.at[o], dr.at[o], zpeer(o))

    pl.semaphore_wait(barrier, len(peers))

    rows_direct, rows_onward = gather(phon_part, ps, pr)
    cols_direct, cols_onward = gather(w2_part, ws, wr)
    durs = [dur_copy(o) for o in range(1, NZ)]
    for o in DIRECT:
        cols_direct[o].start()
    for o in DIRECT:
        rows_direct[o].start()
    for d in durs:
        d.start()
    for o in (5, 11, 2, 14):
        cols_direct[o].wait_recv()
        for d in cols_onward[o]:
            d.start()
        rows_direct[o].wait_recv()
        for d in rows_onward[o]:
            d.start()

    def wait_rows(o):
        for held, jobs in ONWARD.items():
            for job, d in zip(jobs, rows_onward[held]):
                if job[1] == o:
                    d.wait_recv()

    def products(j):
        rows = phon[4 * j:4 * j + 4].reshape(64, 1024)
        for k in range(0, TAPS, 2):
            taps = [w[t] for t in range(k, min(k + 2, TAPS))]
            cols = jnp.concatenate(taps, axis=1) if len(taps) > 1 else taps[0]
            prod = jnp.dot(rows, cols, preferred_element_type=F32)
            high = prod.astype(BF)
            low = (prod - high.astype(F32)).astype(BF)
            width = 128 * len(taps)
            zc[64 * j:64 * j + 64, 128 * k:128 * k + width] = high
            zc[256 + 64 * j:256 + 64 * j + 64, 128 * k:128 * k + width] = low

    w_copy.wait()
    rows_direct[1].wait_recv()
    rows_direct[15].wait_recv()
    products(0)

    cols_direct[1].wait_recv()
    cols_direct[15].wait_recv()
    for jobs in cols_onward.values():
        for d in jobs:
            d.wait_recv()
    first = ([remote(w2.at[y, x, c, 0], w2.at[y, x, c, 0], xs.at[d], xr.at[d], xpeer(d)) for d in (1, 2, 3)]
             + [remote(w2.at[y, x, c, 1], w2.at[y, x, c, 1], xs.at[3 + d], xr.at[3 + d], ypeer(d)) for d in (1, 2, 3)])
    for i in (0, 2, 1, 3, 5, 4):
        first[i].start()

    wait_rows(3)
    products(1)

    for d in durs:
        d.wait_recv()
    lengths = jnp.concatenate([dur_all[o] for o in range(NZ)], axis=0).astype(F32).astype(BF)
    col = lax.broadcasted_iota(jnp.int32, (1, 256), 1)
    slot, place = col // 16, lax.rem(col, 16)
    col_off = jnp.zeros_like(col)
    for i, o in enumerate(ORDER):
        col_off = jnp.where(slot == i, o, col_off)
    col_chunk = lax.rem(z + NZ - col_off, NZ)
    row_chunk = lax.rem(z + NZ - lax.broadcasted_iota(jnp.int32, (NZ, 256), 0), NZ)
    lane = lax.broadcasted_iota(jnp.int32, (128, 256), 0)
    upto = ((lane <= place) & (lane < 16)).astype(F32).astype(BF)
    exact = (lane == place).astype(F32).astype(BF)
    whole = (lane < 16).astype(F32).astype(BF)
    within = jnp.dot(lengths, upto, preferred_element_type=F32)
    single = jnp.dot(lengths, exact, preferred_element_type=F32)
    total = jnp.dot(lengths, whole, preferred_element_type=F32)
    same = row_chunk == col_chunk
    ends = jnp.sum(jnp.where(same, within, jnp.where(row_chunk < col_chunk, total, 0.0)), axis=0, keepdims=True)
    sizes = jnp.sum(jnp.where(same, single, 0.0), axis=0, keepdims=True)
    starts = ends - sizes

    def one_hot(first, count):
        frame = (lax.broadcasted_iota(jnp.int32, (count, 256), 0) + first).astype(F32)
        return jnp.where((frame >= starts) & (frame < ends), 1.0, 0.0).astype(BF)

    for j in (2, 3):
        for o in ORDER[4 * j:4 * j + 4]:
            wait_rows(o)
        products(j)

    def hidden(o):
        block = lax.rem(z + o, NZ)
        pick = one_hot(block * 128 - HALO, ROWS)
        pick = jnp.concatenate([pick, pick], axis=1)
        total = jnp.zeros((128, 128), F32)
        for k in range(0, TAPS, 2):
            width = 128 * min(2, TAPS - k)
            got = jnp.dot(pick, zc[:, 128 * k:128 * k + width], preferred_element_type=F32)
            total = total + got[k:k + 128, 0:128]
            if width > 128:
                total = total + got[k + 1:k + 129, 128:256]
        return jnp.maximum(total, 0.0).astype(BF)

    def hid_copy(o):
        return remote(hid_out.at[o], hid_in.at[o], hs.at[o], hr.at[o], zpeer(o))

    def send_hidden(i, carry):
        o = lax.rem(8 + 7 * i, NZ)
        hid_out[o] = hidden(o)
        hid_copy(o).start()
        return carry

    lax.fori_loop(0, 4, send_hidden, 0)

    for d in first:
        d.wait_recv()
    second = ([remote(w2.at[y, :, c, 0], w2.at[y, :, c, 0], xs.at[6 + d], xr.at[6 + d], ypeer(d)) for d in (1, 2, 3)]
              + [remote(w2.at[:, x, c, 1], w2.at[:, x, c, 1], xs.at[9 + d], xr.at[9 + d], xpeer(d)) for d in (1, 2, 3)])
    for i in (0, 2, 1, 3, 5, 4):
        second[i].start()

    def to_sibling(i):
        if i < 4:
            part = w2.at[lax.rem(y + 4 - i, 4), :, c, 0]
        else:
            part = w2.at[:, lax.rem(x + 8 - i, 4), c, 1]
        return remote(part, part, cs.at[i], cr.at[i], sibling)

    cross = [to_sibling(i) for i in range(8)]
    cross[0].start()
    cross[4].start()

    lax.fori_loop(4, 8, send_hidden, 0)
    lax.fori_loop(9, NZ, send_hidden, 0)
    hid_in[0] = hidden(0)

    acc[...] = jnp.dot(one_hot(z * 128, 128), phon[...].reshape(256, 1024), preferred_element_type=F32)

    for i in (1, 3, 2):
        second[i - 1].wait_recv()
        cross[i].start()
        second[2 + i].wait_recv()
        cross[4 + i].start()
    for d in cross:
        d.wait_recv()

    order = [(8 + 7 * i) % NZ for i in range(NZ)]
    groups = (order[0:4], order[4:8], [0] + order[9:12], order[12:16])
    for group in groups:
        for o in group:
            if o:
                hid_copy(o).wait_recv()
        left = jnp.concatenate([hid_in[o] for o in group], axis=1)
        slots = [ORDER.index(o) for o in group]
        right = jnp.concatenate(
            [w2[:, :, :, :, :, 128 * i:128 * i + 128].reshape(1024, 128) for i in slots], axis=1)
        acc[...] += lax.dot_general(left, right, (((1,), (1,)), ((), ())), preferred_element_type=F32)

    gain_copy.wait()

    def norm(i, carry):
        rows = pl.ds(pl.multiple_of(i * 16, 16), 16)
        summed = acc[rows, :]
        centered = summed - jnp.mean(summed, axis=-1, keepdims=True)
        spread = jnp.mean(centered * centered, axis=-1, keepdims=True)
        out[0, rows, :] = (centered * lax.rsqrt(spread + 1e-5) * gain[...]).astype(BF)
        return carry

    lax.fori_loop(0, 8, norm, 0)

    for o in DIRECT:
        rows_direct[o].wait_send()
        cols_direct[o].wait_send()
    for jobs in [*rows_onward.values(), *cols_onward.values()]:
        for d in jobs:
            d.wait_send()
    for d in durs + first + second + cross:
        d.wait_send()
    for o in range(1, NZ):
        hid_copy(o).wait_send()


def on_device(phonemes, durations, conv_weight, out_weight, norm_gain):
    vmem = pl.BlockSpec(memory_space=pltpu.VMEM)
    sems = pltpu.SemaphoreType.DMA
    return pl.pallas_call(
        kernel,
        out_shape=jax.ShapeDtypeStruct((1, 128, 1024), BF),
        in_specs=[pl.BlockSpec(memory_space=pltpu.HBM)] * 5,
        out_specs=vmem,
        scratch_shapes=[
            pltpu.VMEM((NZ, 16, 1024), BF),
            pltpu.VMEM((1, 16), jnp.int32),
            pltpu.VMEM((1, 128), jnp.int32),
            pltpu.VMEM((NZ, 1, 128), jnp.int32),
            pltpu.VMEM((TAPS, 1024, 128), BF),
            pltpu.VMEM((32, 128), BF),
            pltpu.VMEM((1, 1024), F32),
            pltpu.VMEM((512, TAPS * 128), BF),
            pltpu.VMEM((4, 4, 2, 2, 16, 2048), BF),
            pltpu.VMEM((NZ, 128, 128), BF),
            pltpu.VMEM((NZ, 128, 128), BF),
            pltpu.VMEM((128, 1024), F32),
            sems((5,)), sems((16,)), sems((16,)), sems((16,)), sems((16,)), sems((16,)), sems((16,)),
            sems((13,)), sems((13,)), sems((8,)), sems((8,)), sems((16,)), sems((16,)),
        ],
        compiler_params=pltpu.CompilerParams(
            collective_id=0, has_side_effects=True, vmem_limit_bytes=63 * 1024 * 1024),
        cost_estimate=pl.CostEstimate(flops=4_000_000_000, bytes_accessed=4_000_000, transcendentals=0),
    )(phonemes, durations, conv_weight, out_weight.T, norm_gain.reshape(1, 1024))


def solution(mesh):
    placed = (P("dp", "tm", None), P("dp", "tm"), P(None, None, "tm"), P("tm", "dp"), P())
    return jax.shard_map(
        on_device, mesh=mesh, in_specs=placed, out_specs=P("dp", "tm", None), check_vma=False
    )
```

```python
import jax
import jax.numpy as jnp
from jax import lax
from jax.experimental import pallas as pl
from jax.experimental.pallas import tpu as pltpu
from jax.sharding import PartitionSpec as P

MESH = pl.DeviceIdType.MESH
BF, F32 = jnp.bfloat16, jnp.float32
NZ = 16
ORDER = (0, 1, 15, 3, 13, 4, 12, 2, 14, 6, 10, 7, 9, 5, 11, 8)
DIRECT = (3, 13, 1, 15)
ONWARD = {3: ((3, 6), (1, 4), (15, 2)), 13: ((13, 10), (15, 12), (1, 14)),
          6: ((2, 8), (1, 7), (15, 5)), 10: ((14, 8), (15, 9), (1, 11))}
GROUPS = ((0, 5), (5, 11), (11, 16))
WAVES = ((0, 11), (11, 16))
TAPS = 9
HALO = TAPS // 2
ROWS = 144


def kernel(phon_in, dur_in, conv_w, out_w, gain_in, out,
           phon, dur_row, dur_all, w, w2_own, gain, zc, w2, hid_out, hid_in, acc,
           in_sem, ps, pr, ds, dr, ws, wr, xs, xr, cs, cr, hs, hr):
    z = lax.axis_index("tm")
    dp = lax.axis_index("dp")
    y, x, c = dp // 8, lax.rem(dp // 2, 4), lax.rem(dp, 2)

    def zpeer(o):
        return (dp, lax.rem(z + o, NZ))

    def xpeer(d):
        return (y * 8 + lax.rem(x + d, 4) * 2 + c, z)

    def ypeer(d):
        return (lax.rem(y + d, 4) * 8 + x * 2 + c, z)

    sibling = (y * 8 + x * 2 + 1 - c, z)

    def remote(src, dst, ssem, rsem, dev):
        return pltpu.make_async_remote_copy(
            src_ref=src, dst_ref=dst, send_sem=ssem, recv_sem=rsem, device_id=dev, device_id_type=MESH)

    barrier = pltpu.get_barrier_semaphore()
    peers = [zpeer(o) for o in (1, 2, 3, 13, 14, 15)] + [xpeer(d) for d in (1, 2, 3)] + [ypeer(d) for d in (1, 2, 3)] + [sibling]
    for dev in peers:
        pl.semaphore_signal(barrier, inc=1, device_id=dev, device_id_type=MESH)

    phon_copy = pltpu.make_async_copy(phon_in.at[0], phon.at[0], in_sem.at[0])
    dur_load = pltpu.make_async_copy(dur_in, dur_row, in_sem.at[1])
    w2_copy = pltpu.make_async_copy(out_w, w2_own, in_sem.at[2])
    gain_copy = pltpu.make_async_copy(gain_in, gain, in_sem.at[3])
    w_copy = pltpu.make_async_copy(conv_w, w, in_sem.at[4])
    for d in (phon_copy, dur_load, w2_copy, gain_copy, w_copy):
        d.start()

    dur_all[0] = jnp.zeros((1, 128), jnp.int32)
    dur_load.wait()
    dur_all[0, :, 0:16] = dur_row[...]
    w2_copy.wait()
    w2[y, x, c, 0, :, 0:128] = w2_own[0:16]
    w2[y, x, c, 1, :, 0:128] = w2_own[16:32]
    phon_copy.wait()

    def phon_part(o, part):
        if part is None:
            return phon.at[ORDER.index(o)]
        return phon.at[ORDER.index(o), :, pl.ds(512 * part, 512)]

    def w2_part(o, part):
        lanes = pl.ds(128 * ORDER.index(o), 128)
        if part is None:
            return w2.at[y, x, c, :, :, lanes]
        return w2.at[y, x, c, part, :, lanes]

    def dur_part(o, part):
        return dur_all.at[o]

    def gather(place, ssem, rsem, halves=True):
        def copy(held, to, there):
            part = None if there != 8 or not halves else (0 if held == 6 else 1)
            i = 0 if part == 1 else there
            return remote(place(held, part), place(there, part), ssem.at[i], rsem.at[i], zpeer(to))

        direct = {o: [copy(0, o, o)] for o in DIRECT}
        onward = {held: [copy(held, to, there) for to, there in jobs if halves or (held, there) != (10, 8)]
                  for held, jobs in ONWARD.items()}
        arrival = dict(direct)
        for held, jobs in ONWARD.items():
            for job, d in zip(jobs[::-1], onward[held][::-1]):
                arrival[job[1]] = arrival.get(job[1], []) + [d]
        return direct, onward, arrival

    pl.semaphore_wait(barrier, len(peers))

    gathers = [gather(w2_part, ws, wr), gather(phon_part, ps, pr), gather(dur_part, ds, dr, False)]
    cols, rows, durs = [g[2] for g in gathers]

    def arrive(chunks, which):
        for o in which:
            for d in chunks.pop(o, []):
                d.wait_recv()

    for direct, _, _ in gathers:
        for o in DIRECT:
            direct[o][0].start()
    for held in ONWARD:
        for _, onward, arrival in gathers:
            arrive(arrival, (held,))
            for d in onward[held]:
                d.start()

    def products(begin, end):
        rows = phon[begin:end].reshape(16 * (end - begin), 1024)
        for k in range(0, TAPS, 2):
            taps = [w[t] for t in range(k, min(k + 2, TAPS))]
            cols = jnp.concatenate(taps, axis=1) if len(taps) > 1 else taps[0]
            prod = jnp.dot(rows, cols, preferred_element_type=F32)
            high = prod.astype(BF)
            low = (prod - high.astype(F32)).astype(BF)
            width = 128 * len(taps)
            zc[16 * begin:16 * end, 128 * k:128 * k + width] = high
            zc[256 + 16 * begin:256 + 16 * end, 128 * k:128 * k + width] = low

    def spread(i):
        lanes = pl.ds(128 * WAVES[i][0], 128 * (WAVES[i][1] - WAVES[i][0]))
        first, second, cross = [], [], []
        own = [w2.at[y, x, c, h, :, lanes] for h in (0, 1)]
        row, column = w2.at[y, :, c, 0, :, lanes], w2.at[:, x, c, 1, :, lanes]
        for d in (1, 3, 2):
            first.append(remote(own[0], own[0], xs.at[i, d], xr.at[i, d], xpeer(d)))
            first.append(remote(own[1], own[1], xs.at[i, 3 + d], xr.at[i, 3 + d], ypeer(d)))
            second.append(remote(row, row, xs.at[i, 6 + d], xr.at[i, 6 + d], ypeer(d)))
            second.append(remote(column, column, xs.at[i, 9 + d], xr.at[i, 9 + d], xpeer(d)))
        for d in (0, 1, 3, 2):
            part = w2.at[lax.rem(y + 4 - d, 4), :, c, 0, :, lanes]
            cross.append(remote(part, part, cs.at[i, d], cr.at[i, d], sibling))
            part = w2.at[:, lax.rem(x + 4 - d, 4), c, 1, :, lanes]
            cross.append(remote(part, part, cs.at[i, 4 + d], cr.at[i, 4 + d], sibling))
        return first, second, cross

    spreads = [spread(i) for i in range(len(WAVES))]

    def spread_first(i):
        arrive(cols, ORDER[WAVES[i][0]:WAVES[i][1]])
        for d in spreads[i][0]:
            d.start()

    def spread_second(i):
        first, second, cross = spreads[i]
        for d in first:
            d.wait_recv()
        for d in second + cross[0:2]:
            d.start()

    def spread_cross(i):
        _, second, cross = spreads[i]
        for d, onward in zip(second, cross[2:]):
            d.wait_recv()
            onward.start()

    spread_first(0)
    w_copy.wait()
    for begin, end in GROUPS[0:2]:
        arrive(rows, ORDER[begin:end])
        products(begin, end)
    spread_first(1)

    arrive(durs, range(NZ))
    lengths = jnp.concatenate([dur_all[o] for o in range(NZ)], axis=0).astype(F32).astype(BF)
    col = lax.broadcasted_iota(jnp.int32, (1, 256), 1)
    slot, place = col // 16, lax.rem(col, 16)
    col_off = jnp.zeros_like(col)
    for i, o in enumerate(ORDER):
        col_off = jnp.where(slot == i, o, col_off)
    col_chunk = lax.rem(z + NZ - col_off, NZ)
    row_chunk = lax.rem(z + NZ - lax.broadcasted_iota(jnp.int32, (NZ, 256), 0), NZ)
    lane = lax.broadcasted_iota(jnp.int32, (128, 256), 0)
    upto = ((lane <= place) & (lane < 16)).astype(F32).astype(BF)
    exact = (lane == place).astype(F32).astype(BF)
    whole = (lane < 16).astype(F32).astype(BF)
    within = jnp.dot(lengths, upto, preferred_element_type=F32)
    single = jnp.dot(lengths, exact, preferred_element_type=F32)
    total = jnp.dot(lengths, whole, preferred_element_type=F32)
    same = row_chunk == col_chunk
    ends = jnp.sum(jnp.where(same, within, jnp.where(row_chunk < col_chunk, total, 0.0)), axis=0, keepdims=True)
    sizes = jnp.sum(jnp.where(same, single, 0.0), axis=0, keepdims=True)
    starts = ends - sizes

    def one_hot(first, count):
        frame = (lax.broadcasted_iota(jnp.int32, (count, 256), 0) + first).astype(F32)
        return jnp.where((frame >= starts) & (frame < ends), 1.0, 0.0).astype(BF)

    begin, end = GROUPS[2]
    arrive(rows, ORDER[begin:end])
    products(begin, end)

    def hidden(o):
        block = lax.rem(z + o, NZ)
        pick = one_hot(block * 128 - HALO, ROWS)
        pick = jnp.concatenate([pick, pick], axis=1)
        total = jnp.zeros((128, 128), F32)
        for k in range(0, TAPS, 2):
            width = 128 * min(2, TAPS - k)
            got = jnp.dot(pick, zc[:, 128 * k:128 * k + width], preferred_element_type=F32)
            total = total + got[k:k + 128, 0:128]
            if width > 128:
                total = total + got[k + 1:k + 129, 128:256]
        return jnp.maximum(total, 0.0).astype(BF)

    def hid_copy(o):
        return remote(hid_out.at[o], hid_in.at[o], hs.at[o], hr.at[o], zpeer(o))

    def send_hidden(i, carry):
        o = lax.rem(8 + 7 * i, NZ)
        hid_out[o] = hidden(o)
        hid_copy(o).start()
        return carry

    lax.fori_loop(0, 3, send_hidden, 0)
    spread_second(0)
    lax.fori_loop(3, 6, send_hidden, 0)
    spread_second(1)
    lax.fori_loop(6, 8, send_hidden, 0)
    lax.fori_loop(9, NZ, send_hidden, 0)
    hid_in[0] = hidden(0)

    acc[...] = jnp.dot(one_hot(z * 128, 128), phon[...].reshape(256, 1024), preferred_element_type=F32)

    for i in range(len(WAVES)):
        spread_cross(i)
    for _, _, cross in spreads:
        for d in cross:
            d.wait_recv()

    order = [(8 + 7 * i) % NZ for i in range(NZ)]
    groups = (order[0:4], order[4:8], [0] + order[9:12], order[12:16])
    for group in groups:
        for o in group:
            if o:
                hid_copy(o).wait_recv()
        left = jnp.concatenate([hid_in[o] for o in group], axis=1)
        slots = [ORDER.index(o) for o in group]
        right = jnp.concatenate(
            [w2[:, :, :, :, :, 128 * i:128 * i + 128].reshape(1024, 128) for i in slots], axis=1)
        acc[...] += lax.dot_general(left, right, (((1,), (1,)), ((), ())), preferred_element_type=F32)

    gain_copy.wait()

    def norm(i, carry):
        rows = pl.ds(pl.multiple_of(i * 16, 16), 16)
        summed = acc[rows, :]
        centered = summed - jnp.mean(summed, axis=-1, keepdims=True)
        spread = jnp.mean(centered * centered, axis=-1, keepdims=True)
        out[0, rows, :] = (centered * lax.rsqrt(spread + 1e-5) * gain[...]).astype(BF)
        return carry

    lax.fori_loop(0, 8, norm, 0)

    for direct, onward, _ in gathers:
        for jobs in [*direct.values(), *onward.values()]:
            for d in jobs:
                d.wait_send()
    for first, second, cross in spreads:
        for d in first + second + cross:
            d.wait_send()
    for o in range(1, NZ):
        hid_copy(o).wait_send()


def on_device(phonemes, durations, conv_weight, out_weight, norm_gain):
    vmem = pl.BlockSpec(memory_space=pltpu.VMEM)
    sems = pltpu.SemaphoreType.DMA
    return pl.pallas_call(
        kernel,
        out_shape=pltpu.VMEM((1, 128, 1024), BF),
        in_specs=[pl.BlockSpec(memory_space=pltpu.HBM)] * 5,
        out_specs=vmem,
        scratch_shapes=[
            pltpu.VMEM((NZ, 16, 1024), BF),
            pltpu.VMEM((1, 16), jnp.int32),
            pltpu.VMEM((NZ, 1, 128), jnp.int32),
            pltpu.VMEM((TAPS, 1024, 128), BF),
            pltpu.VMEM((32, 128), BF),
            pltpu.VMEM((1, 1024), F32),
            pltpu.VMEM((512, TAPS * 128), BF),
            pltpu.VMEM((4, 4, 2, 2, 16, 2048), BF),
            pltpu.VMEM((NZ, 128, 128), BF),
            pltpu.VMEM((NZ, 128, 128), BF),
            pltpu.VMEM((128, 1024), F32),
            sems((5,)), sems((16,)), sems((16,)), sems((16,)), sems((16,)), sems((16,)), sems((16,)),
            sems((2, 13)), sems((2, 13)), sems((2, 8)), sems((2, 8)), sems((16,)), sems((16,)),
        ],
        compiler_params=pltpu.CompilerParams(
            collective_id=0, has_side_effects=True, vmem_limit_bytes=63 * 1024 * 1024),
        cost_estimate=pl.CostEstimate(flops=4_000_000_000, bytes_accessed=4_000_000, transcendentals=0),
    )(phonemes, durations, conv_weight, out_weight.T, norm_gain.reshape(1, 1024))


def solution(mesh):
    placed = (P("dp", "tm", None), P("dp", "tm"), P(None, None, "tm"), P("tm", "dp"), P())
    return jax.shard_map(
        on_device, mesh=mesh, in_specs=placed, out_specs=P("dp", "tm", None), check_vma=False
    )
```

```python
import jax
import jax.numpy as jnp
from jax import lax
from jax.experimental import pallas as pl
from jax.experimental.pallas import tpu as pltpu
from jax.sharding import PartitionSpec as P

MESH = pl.DeviceIdType.MESH
BF, F32 = jnp.bfloat16, jnp.float32
NZ = 16
ORDER = (0, 1, 15, 3, 13, 4, 12, 2, 14, 6, 10, 7, 9, 5, 11, 8)
DIRECT = (3, 13, 1, 15)
ONWARD = {3: ((3, 6), (1, 4), (15, 2)), 13: ((13, 10), (15, 12), (1, 14)),
          6: ((2, 8), (1, 7), (15, 5)), 10: ((14, 8), (15, 9), (1, 11))}
GREETED = (1, 2, 3, 13, 14, 15)
GROUPS = ((0, 5), (5, 11), (11, 16))
WAVES = ((0, 11), (11, 16))
TAPS = 9
HALO = TAPS // 2
ROWS = 144


def kernel(phon_in, dur_in, conv_w, out_w, gain_in, out,
           phon, dur_row, dur_wide, w, w2_own, gain, zc, w2, hid_out, hid_in, acc,
           in_sem, ps, pr, ws, wr, xs, xr, cs, cr, hs, hr):
    z = lax.axis_index("tm")
    dp = lax.axis_index("dp")
    y, x, c = dp // 8, lax.rem(dp // 2, 4), lax.rem(dp, 2)

    def zpeer(o):
        return (dp, lax.rem(z + o, NZ))

    def xpeer(d):
        return (y * 8 + lax.rem(x + d, 4) * 2 + c, z)

    def ypeer(d):
        return (lax.rem(y + d, 4) * 8 + x * 2 + c, z)

    sibling = (y * 8 + x * 2 + 1 - c, z)

    def remote(src, dst, ssem, rsem, dev):
        return pltpu.make_async_remote_copy(
            src_ref=src, dst_ref=dst, send_sem=ssem, recv_sem=rsem, device_id=dev, device_id_type=MESH)

    barrier = pltpu.get_barrier_semaphore()
    peers = [zpeer(o) for o in GREETED] + [xpeer(d) for d in (1, 2, 3)] + [ypeer(d) for d in (1, 2, 3)] + [sibling]
    for dev in peers:
        pl.semaphore_signal(barrier, inc=1, device_id=dev, device_id_type=MESH)

    phon_copy = pltpu.make_async_copy(phon_in.at[0], phon.at[0, :, pl.ds(0, 1024)], in_sem.at[0])
    dur_load = pltpu.make_async_copy(dur_in, dur_row, in_sem.at[1])
    w2_copy = pltpu.make_async_copy(out_w, w2_own, in_sem.at[2])
    gain_copy = pltpu.make_async_copy(gain_in, gain, in_sem.at[3])
    w_copy = pltpu.make_async_copy(conv_w, w, in_sem.at[4])
    for d in (phon_copy, dur_load, w2_copy, gain_copy, w_copy):
        d.start()

    dur_wide[...] = jnp.zeros_like(dur_wide)
    dur_load.wait()
    dur_wide[:, 0:16] = dur_row[...]
    top = lax.broadcasted_iota(jnp.int32, (16, 128), 0) == 0
    phon[0, :, 1024:1152] = jnp.where(top, dur_wide[...].astype(F32), 0.0).astype(BF)
    w2_copy.wait()
    w2[y, x, c, 0, :, 0:128] = w2_own[0:16]
    w2[y, x, c, 1, :, 0:128] = w2_own[16:32]
    phon_copy.wait()

    def phon_part(o, part):
        if part is None:
            return phon.at[ORDER.index(o)]
        return phon.at[ORDER.index(o), :, pl.ds(640 * part, 640 - 128 * part)]

    def w2_part(o, part):
        lanes = pl.ds(128 * ORDER.index(o), 128)
        if part is None:
            return w2.at[y, x, c, :, :, lanes]
        return w2.at[y, x, c, part, :, lanes]

    def gather(place, ssem, rsem):
        def copy(held, to, there):
            part = None if there != 8 else (0 if held < 8 else 1)
            i = 0 if part == 1 else there
            return remote(place(held, part), place(there, part), ssem.at[i], rsem.at[i], zpeer(to))

        direct = {o: [copy(0, o, o)] for o in DIRECT}
        onward = {held: [copy(held, to, there) for to, there in jobs] for held, jobs in ONWARD.items()}
        arrival = dict(direct)
        for held, jobs in ONWARD.items():
            for job, d in zip(jobs, onward[held]):
                arrival[job[1]] = arrival.get(job[1], []) + [d]
        return direct, onward, arrival

    pl.semaphore_wait(barrier, len(peers))

    gathers = [gather(phon_part, ps, pr), gather(w2_part, ws, wr)]
    rows, cols = [g[2] for g in gathers]

    def arrive(chunks, which):
        for o in which:
            for d in chunks.pop(o, []):
                d.wait_recv()

    for direct, _, _ in gathers:
        for o in DIRECT:
            direct[o][0].start()
    for helds in (DIRECT[0:2], (6, 10)):
        for _, onward, arrival in gathers:
            for held in helds:
                arrive(arrival, (held,))
                for d in onward[held]:
                    d.start()

    def products(begin, end):
        rows = phon[begin:end, :, 0:1024].reshape(16 * (end - begin), 1024)
        for k in range(0, TAPS, 2):
            taps = [w[t] for t in range(k, min(k + 2, TAPS))]
            cols = jnp.concatenate(taps, axis=1) if len(taps) > 1 else taps[0]
            prod = jnp.dot(rows, cols, preferred_element_type=F32)
            high = prod.astype(BF)
            low = (prod - high.astype(F32)).astype(BF)
            width = 128 * len(taps)
            zc[16 * begin:16 * end, 128 * k:128 * k + width] = high
            zc[256 + 16 * begin:256 + 16 * end, 128 * k:128 * k + width] = low

    def spread(i):
        lanes = pl.ds(128 * WAVES[i][0], 128 * (WAVES[i][1] - WAVES[i][0]))
        first, second, cross = [], [], []
        own = [w2.at[y, x, c, h, :, lanes] for h in (0, 1)]
        row, column = w2.at[y, :, c, 0, :, lanes], w2.at[:, x, c, 1, :, lanes]
        for d in (1, 3, 2):
            first.append(remote(own[0], own[0], xs.at[i, d], xr.at[i, d], xpeer(d)))
            first.append(remote(own[1], own[1], xs.at[i, 3 + d], xr.at[i, 3 + d], ypeer(d)))
            second.append(remote(row, row, xs.at[i, 6 + d], xr.at[i, 6 + d], ypeer(d)))
            second.append(remote(column, column, xs.at[i, 9 + d], xr.at[i, 9 + d], xpeer(d)))
        for d in (0, 1, 3, 2):
            part = w2.at[lax.rem(y + 4 - d, 4), :, c, 0, :, lanes]
            cross.append(remote(part, part, cs.at[i, d], cr.at[i, d], sibling))
            part = w2.at[:, lax.rem(x + 4 - d, 4), c, 1, :, lanes]
            cross.append(remote(part, part, cs.at[i, 4 + d], cr.at[i, 4 + d], sibling))
        return first, second, cross

    spreads = [spread(i) for i in range(len(WAVES))]

    def spread_first(i):
        arrive(cols, ORDER[WAVES[i][0]:WAVES[i][1]])
        for d in spreads[i][0]:
            d.start()

    def spread_second(i):
        first, second, cross = spreads[i]
        for d in first:
            d.wait_recv()
        for d in second + cross[0:2]:
            d.start()

    def spread_cross(i):
        _, second, cross = spreads[i]
        for d, onward in zip(second, cross[2:]):
            d.wait_recv()
            onward.start()

    w_copy.wait()
    for begin, end in GROUPS[0:2]:
        arrive(rows, ORDER[begin:end])
        products(begin, end)
    spread_first(0)

    begin, end = GROUPS[2]
    arrive(rows, ORDER[begin:end])
    chunk = lax.broadcasted_iota(jnp.int32, (NZ, 256), 0)
    line = lax.broadcasted_iota(jnp.int32, (NZ, 256), 1)
    pick_line = jnp.zeros((NZ, 256), F32)
    for i, o in enumerate(ORDER):
        pick_line = jnp.where((chunk == o) & (line == 16 * i), 1.0, pick_line)
    lengths = jnp.dot(pick_line.astype(BF), phon[:, :, 1024:1152].reshape(256, 128),
                      preferred_element_type=F32).astype(BF)
    col = lax.broadcasted_iota(jnp.int32, (1, 256), 1)
    slot, place = col // 16, lax.rem(col, 16)
    col_off = jnp.zeros_like(col)
    for i, o in enumerate(ORDER):
        col_off = jnp.where(slot == i, o, col_off)
    col_chunk = lax.rem(z + NZ - col_off, NZ)
    row_chunk = lax.rem(z + NZ - lax.broadcasted_iota(jnp.int32, (NZ, 256), 0), NZ)
    lane = lax.broadcasted_iota(jnp.int32, (128, 256), 0)
    upto = ((lane <= place) & (lane < 16)).astype(F32).astype(BF)
    exact = (lane == place).astype(F32).astype(BF)
    whole = (lane < 16).astype(F32).astype(BF)
    within = jnp.dot(lengths, upto, preferred_element_type=F32)
    single = jnp.dot(lengths, exact, preferred_element_type=F32)
    total = jnp.dot(lengths, whole, preferred_element_type=F32)
    same = row_chunk == col_chunk
    ends = jnp.sum(jnp.where(same, within, jnp.where(row_chunk < col_chunk, total, 0.0)), axis=0, keepdims=True)
    sizes = jnp.sum(jnp.where(same, single, 0.0), axis=0, keepdims=True)
    starts = ends - sizes

    def one_hot(first, count):
        frame = (lax.broadcasted_iota(jnp.int32, (count, 256), 0) + first).astype(F32)
        return jnp.where((frame >= starts) & (frame < ends), 1.0, 0.0).astype(BF)

    products(begin, end)

    def hidden(o):
        block = lax.rem(z + o, NZ)
        pick = one_hot(block * 128 - HALO, ROWS)
        pick = jnp.concatenate([pick, pick], axis=1)
        total = jnp.zeros((128, 128), F32)
        for k in range(0, TAPS, 2):
            width = 128 * min(2, TAPS - k)
            got = jnp.dot(pick, zc[:, 128 * k:128 * k + width], preferred_element_type=F32)
            total = total + got[k:k + 128, 0:128]
            if width > 128:
                total = total + got[k + 1:k + 129, 128:256]
        return jnp.maximum(total, 0.0).astype(BF)

    def hid_copy(o):
        return remote(hid_out.at[o], hid_in.at[o], hs.at[o], hr.at[o], zpeer(o))

    def send_hidden(i, carry):
        o = lax.rem(8 + 7 * i, NZ)
        hid_out[o] = hidden(o)
        hid_copy(o).start()
        return carry

    lax.fori_loop(0, 4, send_hidden, 0)
    spread_first(1)
    lax.fori_loop(4, 8, send_hidden, 0)
    lax.fori_loop(9, NZ, send_hidden, 0)
    spread_second(0)
    spread_second(1)
    hid_in[0] = hidden(0)

    acc[...] = jnp.dot(one_hot(z * 128, 128), phon[:, :, 0:1024].reshape(256, 1024), preferred_element_type=F32)

    for i in range(len(WAVES)):
        spread_cross(i)
    for _, _, cross in spreads:
        for d in cross:
            d.wait_recv()

    order = [(8 + 7 * i) % NZ for i in range(NZ)]
    groups = (order[0:4], order[4:8], [0] + order[9:12], order[12:14], order[14:16])
    for group in groups:
        for o in group:
            if o:
                hid_copy(o).wait_recv()
        left = jnp.concatenate([hid_in[o] for o in group], axis=1)
        slots = [ORDER.index(o) for o in group]
        right = jnp.concatenate(
            [w2[:, :, :, :, :, 128 * i:128 * i + 128].reshape(1024, 128) for i in slots], axis=1)
        acc[...] += lax.dot_general(left, right, (((1,), (1,)), ((), ())), preferred_element_type=F32)

    gain_copy.wait()

    def norm(i, carry):
        rows = pl.ds(pl.multiple_of(i * 16, 16), 16)
        summed = acc[rows, :]
        centered = summed - jnp.mean(summed, axis=-1, keepdims=True)
        spread = jnp.mean(centered * centered, axis=-1, keepdims=True)
        out[0, rows, :] = (centered * lax.rsqrt(spread + 1e-5) * gain[...]).astype(BF)
        return carry

    lax.fori_loop(0, 8, norm, 0, unroll=True)

    for direct, onward, _ in gathers:
        for jobs in [*direct.values(), *onward.values()]:
            for d in jobs:
                d.wait_send()
    for first, second, cross in spreads:
        for d in first + second + cross:
            d.wait_send()
    for o in range(1, NZ):
        hid_copy(o).wait_send()


def on_device(phonemes, durations, conv_weight, out_weight, norm_gain):
    vmem = pl.BlockSpec(memory_space=pltpu.VMEM)
    sems = pltpu.SemaphoreType.DMA
    return pl.pallas_call(
        kernel,
        out_shape=pltpu.VMEM((1, 128, 1024), BF),
        in_specs=[pl.BlockSpec(memory_space=pltpu.HBM)] * 5,
        out_specs=vmem,
        scratch_shapes=[
            pltpu.VMEM((NZ, 16, 1152), BF),
            pltpu.VMEM((1, 16), jnp.int32),
            pltpu.VMEM((1, 128), jnp.int32),
            pltpu.VMEM((TAPS, 1024, 128), BF),
            pltpu.VMEM((32, 128), BF),
            pltpu.VMEM((1, 1024), F32),
            pltpu.VMEM((512, TAPS * 128), BF),
            pltpu.VMEM((4, 4, 2, 2, 16, 2048), BF),
            pltpu.VMEM((NZ, 128, 128), BF),
            pltpu.VMEM((NZ, 128, 128), BF),
            pltpu.VMEM((128, 1024), F32),
            sems((5,)), sems((16,)), sems((16,)), sems((16,)), sems((16,)),
            sems((2, 13)), sems((2, 13)), sems((2, 8)), sems((2, 8)), sems((16,)), sems((16,)),
        ],
        compiler_params=pltpu.CompilerParams(
            collective_id=0, has_side_effects=True, vmem_limit_bytes=63 * 1024 * 1024),
        cost_estimate=pl.CostEstimate(flops=4_000_000_000, bytes_accessed=4_000_000, transcendentals=0),
    )(phonemes, durations, conv_weight, out_weight.T, norm_gain.reshape(1, 1024))


def solution(mesh):
    placed = (P("dp", "tm", None), P("dp", "tm"), P(None, None, "tm"), P("tm", "dp"), P())
    return jax.shard_map(
        on_device, mesh=mesh, in_specs=placed, out_specs=P("dp", "tm", None), check_vma=False
    )
```

```python
import jax
import jax.numpy as jnp
from jax import lax
from jax.experimental import pallas as pl
from jax.experimental.pallas import tpu as pltpu
from jax.sharding import PartitionSpec as P

MESH = pl.DeviceIdType.MESH
BF, F32 = jnp.bfloat16, jnp.float32
NZ = 16
ORDER = (0, 1, 15, 3, 13, 4, 12, 2, 14, 6, 10, 7, 9, 5, 11, 8)
DIRECT = (3, 13, 1, 15)
ONWARD = {3: ((3, 6), (1, 4), (15, 2)), 13: ((13, 10), (15, 12), (1, 14)),
          6: ((2, 8), (1, 7), (15, 5)), 10: ((14, 8), (15, 9), (1, 11))}
GREETED = (1, 2, 3, 13, 14, 15)
GROUPS = ((0, 5), (5, 11), (11, 16))
WAVES = ((0, 11), (11, 16))
TAPS = 9
HALO = TAPS // 2
ROWS = 144


def kernel(phon_in, dur_in, conv_w, out_w, gain_in, out,
           phon, dur_row, dur_all, w, w2_own, gain, zc, w2, hid_out, hid_in, acc,
           in_sem, ps, pr, ds, dr, ws, wr, xs, xr, cs, cr, hs, hr):
    z = lax.axis_index("tm")
    dp = lax.axis_index("dp")
    y, x, c = dp // 8, lax.rem(dp // 2, 4), lax.rem(dp, 2)

    def zpeer(o):
        return (dp, lax.rem(z + o, NZ))

    def xpeer(d):
        return (y * 8 + lax.rem(x + d, 4) * 2 + c, z)

    def ypeer(d):
        return (lax.rem(y + d, 4) * 8 + x * 2 + c, z)

    sibling = (y * 8 + x * 2 + 1 - c, z)

    def remote(src, dst, ssem, rsem, dev):
        return pltpu.make_async_remote_copy(
            src_ref=src, dst_ref=dst, send_sem=ssem, recv_sem=rsem, device_id=dev, device_id_type=MESH)

    barrier = pltpu.get_barrier_semaphore()
    around = [zpeer(o) for o in GREETED]
    across = [xpeer(d) for d in (1, 2, 3)] + [ypeer(d) for d in (1, 2, 3)] + [sibling]
    for dev in around:
        pl.semaphore_signal(barrier, inc=1, device_id=dev, device_id_type=MESH)

    phon_copy = pltpu.make_async_copy(phon_in.at[0], phon.at[0], in_sem.at[0])
    dur_load = pltpu.make_async_copy(dur_in, dur_row, in_sem.at[1])
    w2_copy = pltpu.make_async_copy(out_w, w2_own, in_sem.at[2])
    gain_copy = pltpu.make_async_copy(gain_in, gain, in_sem.at[3])
    w_copy = pltpu.make_async_copy(conv_w, w, in_sem.at[4])
    for d in (dur_load, phon_copy, w2_copy, w_copy, gain_copy):
        d.start()
    for dev in across:
        pl.semaphore_signal(barrier, inc=1, device_id=dev, device_id_type=MESH)

    dur_all[0] = jnp.zeros((1, 128), jnp.int32)
    dur_load.wait()
    dur_all[0, :, 0:16] = dur_row[...]
    phon_copy.wait()

    def phon_part(o, part):
        if part is None:
            return phon.at[ORDER.index(o)]
        return phon.at[ORDER.index(o), :, pl.ds(512 * part, 512)]

    def w2_part(o, part):
        lanes = pl.ds(128 * ORDER.index(o), 128)
        if part is None:
            return w2.at[y, x, c, :, :, lanes]
        return w2.at[y, x, c, part, :, lanes]

    def dur_part(o, part):
        return dur_all.at[o]

    def gather(place, ssem, rsem, halves=True):
        def copy(held, to, there):
            part = None if there != 8 or not halves else (0 if held < 8 else 1)
            i = 0 if part == 1 else there
            return remote(place(held, part), place(there, part), ssem.at[i], rsem.at[i], zpeer(to))

        direct = {o: [copy(0, o, o)] for o in DIRECT}
        onward = {held: [copy(held, to, there) for to, there in (jobs if halves or held != 10 else jobs[1:])]
                  for held, jobs in ONWARD.items()}
        arrival = dict(direct)
        for held, jobs in ONWARD.items():
            for job, d in zip(jobs[::-1], onward[held][::-1]):
                arrival[job[1]] = arrival.get(job[1], []) + [d]
        return direct, onward, arrival

    pl.semaphore_wait(barrier, len(around) + len(across))

    gathers = [gather(phon_part, ps, pr), gather(dur_part, ds, dr, False), gather(w2_part, ws, wr)]
    rows, durs, cols = [g[2] for g in gathers]

    def arrive(chunks, which):
        for o in which:
            for d in chunks.pop(o, []):
                d.wait_recv()

    for direct, _, _ in gathers[0:2]:
        for o in DIRECT:
            direct[o][0].start()
    w2_copy.wait()
    w2[y, x, c, 0, :, 0:128] = w2_own[0:16]
    w2[y, x, c, 1, :, 0:128] = w2_own[16:32]
    for o in DIRECT:
        gathers[2][0][o][0].start()
    for helds in (DIRECT[0:2], (6, 10)):
        for _, onward, arrival in gathers:
            for held in helds:
                arrive(arrival, (held,))
                for d in onward[held]:
                    d.start()

    def products(begin, end):
        rows = phon[begin:end].reshape(16 * (end - begin), 1024)
        for k in range(0, TAPS, 2):
            taps = [w[t] for t in range(k, min(k + 2, TAPS))]
            cols = jnp.concatenate(taps, axis=1) if len(taps) > 1 else taps[0]
            prod = jnp.dot(rows, cols, preferred_element_type=F32)
            high = prod.astype(BF)
            low = (prod - high.astype(F32)).astype(BF)
            width = 128 * len(taps)
            zc[16 * begin:16 * end, 128 * k:128 * k + width] = high
            zc[256 + 16 * begin:256 + 16 * end, 128 * k:128 * k + width] = low

    def spread(i):
        lanes = pl.ds(128 * WAVES[i][0], 128 * (WAVES[i][1] - WAVES[i][0]))
        first, second, cross = [], [], []
        own = [w2.at[y, x, c, h, :, lanes] for h in (0, 1)]
        row, column = w2.at[y, :, c, 0, :, lanes], w2.at[:, x, c, 1, :, lanes]
        for d in (1, 3, 2):
            first.append(remote(own[0], own[0], xs.at[i, d], xr.at[i, d], xpeer(d)))
            first.append(remote(own[1], own[1], xs.at[i, 3 + d], xr.at[i, 3 + d], ypeer(d)))
            second.append(remote(row, row, xs.at[i, 6 + d], xr.at[i, 6 + d], ypeer(d)))
            second.append(remote(column, column, xs.at[i, 9 + d], xr.at[i, 9 + d], xpeer(d)))
        for d in (0, 1, 3, 2):
            part = w2.at[lax.rem(y + 4 - d, 4), :, c, 0, :, lanes]
            cross.append(remote(part, part, cs.at[i, d], cr.at[i, d], sibling))
            part = w2.at[:, lax.rem(x + 4 - d, 4), c, 1, :, lanes]
            cross.append(remote(part, part, cs.at[i, 4 + d], cr.at[i, 4 + d], sibling))
        return first, second, cross

    spreads = [spread(i) for i in range(len(WAVES))]

    def spread_first(i):
        arrive(cols, ORDER[WAVES[i][0]:WAVES[i][1]])
        for d in spreads[i][0]:
            d.start()

    def spread_second(i):
        first, second, cross = spreads[i]
        for d in first:
            d.wait_recv()
        for d in second + cross[0:2]:
            d.start()

    def spread_cross(i):
        _, second, cross = spreads[i]
        for d, onward in zip(second, cross[2:]):
            d.wait_recv()
            onward.start()

    w_copy.wait()
    for begin, end in GROUPS[0:2]:
        arrive(rows, ORDER[begin:end])
        products(begin, end)
    spread_first(0)

    arrive(durs, range(NZ))
    lengths = jnp.concatenate([dur_all[o] for o in range(NZ)], axis=0).astype(F32).astype(BF)
    begin, end = GROUPS[2]
    col = lax.broadcasted_iota(jnp.int32, (1, 256), 1)
    slot, place = col // 16, lax.rem(col, 16)
    col_off = jnp.zeros_like(col)
    for i, o in enumerate(ORDER):
        col_off = jnp.where(slot == i, o, col_off)
    col_chunk = lax.rem(z + NZ - col_off, NZ)
    row_chunk = lax.rem(z + NZ - lax.broadcasted_iota(jnp.int32, (NZ, 256), 0), NZ)
    lane = lax.broadcasted_iota(jnp.int32, (128, 256), 0)
    upto = ((lane <= place) & (lane < 16)).astype(F32).astype(BF)
    exact = (lane == place).astype(F32).astype(BF)
    whole = (lane < 16).astype(F32).astype(BF)
    within = jnp.dot(lengths, upto, preferred_element_type=F32)
    single = jnp.dot(lengths, exact, preferred_element_type=F32)
    total = jnp.dot(lengths, whole, preferred_element_type=F32)
    same = row_chunk == col_chunk
    ends = jnp.sum(jnp.where(same, within, jnp.where(row_chunk < col_chunk, total, 0.0)), axis=0, keepdims=True)
    sizes = jnp.sum(jnp.where(same, single, 0.0), axis=0, keepdims=True)
    starts = ends - sizes

    def one_hot(first, count):
        frame = (lax.broadcasted_iota(jnp.int32, (count, 256), 0) + first).astype(F32)
        return jnp.where((frame >= starts) & (frame < ends), 1.0, 0.0).astype(BF)

    arrive(rows, ORDER[begin:end])
    products(begin, end)

    def hidden(o):
        block = lax.rem(z + o, NZ)
        pick = one_hot(block * 128 - HALO, ROWS)
        pick = jnp.concatenate([pick, pick], axis=1)
        total = jnp.zeros((128, 128), F32)
        for k in range(0, TAPS, 2):
            width = 128 * min(2, TAPS - k)
            got = jnp.dot(pick, zc[:, 128 * k:128 * k + width], preferred_element_type=F32)
            total = total + got[k:k + 128, 0:128]
            if width > 128:
                total = total + got[k + 1:k + 129, 128:256]
        return jnp.maximum(total, 0.0).astype(BF)

    def hid_copy(o):
        return remote(hid_out.at[o], hid_in.at[o], hs.at[o], hr.at[o], zpeer(o))

    def send_hidden(i, carry):
        o = lax.rem(8 + 7 * i, NZ)
        hid_out[o] = hidden(o)
        hid_copy(o).start()
        return carry

    lax.fori_loop(0, 4, send_hidden, 0)
    spread_first(1)
    lax.fori_loop(4, 8, send_hidden, 0)
    lax.fori_loop(9, NZ, send_hidden, 0)
    spread_second(0)
    spread_second(1)
    hid_in[0] = hidden(0)

    acc[...] = jnp.dot(one_hot(z * 128, 128), phon[...].reshape(256, 1024), preferred_element_type=F32)

    for i in range(len(WAVES)):
        spread_cross(i)
    for _, _, cross in spreads:
        for d in cross:
            d.wait_recv()

    order = [(8 + 7 * i) % NZ for i in range(NZ)]
    groups = (order[0:4], order[4:8], [0] + order[9:12], order[12:14], order[14:16])
    for group in groups:
        for o in group:
            if o:
                hid_copy(o).wait_recv()
        left = jnp.concatenate([hid_in[o] for o in group], axis=1)
        slots = [ORDER.index(o) for o in group]
        right = jnp.concatenate(
            [w2[:, :, :, :, :, 128 * i:128 * i + 128].reshape(1024, 128) for i in slots], axis=1)
        acc[...] += lax.dot_general(left, right, (((1,), (1,)), ((), ())), preferred_element_type=F32)

    gain_copy.wait()

    def norm(i, carry):
        rows = pl.ds(pl.multiple_of(i * 16, 16), 16)
        summed = acc[rows, :]
        centered = summed - jnp.mean(summed, axis=-1, keepdims=True)
        spread = jnp.mean(centered * centered, axis=-1, keepdims=True)
        out[0, rows, :] = (centered * lax.rsqrt(spread + 1e-5) * gain[...]).astype(BF)
        return carry

    lax.fori_loop(0, 8, norm, 0, unroll=True)

    for direct, onward, _ in gathers:
        for jobs in [*direct.values(), *onward.values()]:
            for d in jobs:
                d.wait_send()
    for first, second, cross in spreads:
        for d in first + second + cross:
            d.wait_send()
    for o in range(1, NZ):
        hid_copy(o).wait_send()


def on_device(phonemes, durations, conv_weight, out_weight, norm_gain):
    vmem = pl.BlockSpec(memory_space=pltpu.VMEM)
    sems = pltpu.SemaphoreType.DMA
    return pl.pallas_call(
        kernel,
        out_shape=pltpu.VMEM((1, 128, 1024), BF),
        in_specs=[pl.BlockSpec(memory_space=pltpu.HBM)] * 5,
        out_specs=vmem,
        scratch_shapes=[
            pltpu.VMEM((NZ, 16, 1024), BF),
            pltpu.VMEM((1, 16), jnp.int32),
            pltpu.VMEM((NZ, 1, 128), jnp.int32),
            pltpu.VMEM((TAPS, 1024, 128), BF),
            pltpu.VMEM((32, 128), BF),
            pltpu.VMEM((1, 1024), F32),
            pltpu.VMEM((512, TAPS * 128), BF),
            pltpu.VMEM((4, 4, 2, 2, 16, 2048), BF),
            pltpu.VMEM((NZ, 128, 128), BF),
            pltpu.VMEM((NZ, 128, 128), BF),
            pltpu.VMEM((128, 1024), F32),
            sems((5,)), sems((16,)), sems((16,)), sems((16,)), sems((16,)), sems((16,)), sems((16,)),
            sems((2, 13)), sems((2, 13)), sems((2, 8)), sems((2, 8)), sems((16,)), sems((16,)),
        ],
        compiler_params=pltpu.CompilerParams(
            collective_id=0, has_side_effects=True, vmem_limit_bytes=63 * 1024 * 1024),
        cost_estimate=pl.CostEstimate(flops=4_000_000_000, bytes_accessed=4_000_000, transcendentals=0),
    )(phonemes, durations, conv_weight, out_weight.T, norm_gain.reshape(1, 1024))


def solution(mesh):
    placed = (P("dp", "tm", None), P("dp", "tm"), P(None, None, "tm"), P("tm", "dp"), P())
    return jax.shard_map(
        on_device, mesh=mesh, in_specs=placed, out_specs=P("dp", "tm", None), check_vma=False
    )
```

```python
import jax
import jax.numpy as jnp
from jax import lax
from jax.experimental import pallas as pl
from jax.experimental.pallas import tpu as pltpu
from jax.sharding import PartitionSpec as P

MESH = pl.DeviceIdType.MESH
BF, F32 = jnp.bfloat16, jnp.float32
NZ = 16
ORDER = (0, 1, 15, 3, 13, 4, 12, 2, 14, 6, 10, 7, 9, 5, 11, 8)
DIRECT = (3, 13, 1, 15)
ONWARD = {3: ((3, 6), (1, 4), (15, 2)), 13: ((13, 10), (15, 12), (1, 14)),
          6: ((2, 8), (1, 7), (15, 5)), 10: ((14, 8), (15, 9), (1, 11))}
GREETED = (1, 2, 3, 13, 14, 15)
GROUPS = ((0, 5), (5, 11), (11, 16))
WAVES = ((0, 11), (11, 16))
TAPS = 9
HALO = TAPS // 2
ROWS = 144


def kernel(phon_in, dur_in, conv_w, out_w, gain_in, out,
           phon, dur_row, dur_all, w, w2_own, gain, zc, w2, hid_out, hid_in, acc,
           in_sem, ps, pr, ds, dr, ws, wr, xs, xr, cs, cr, hs, hr):
    z = lax.axis_index("tm")
    dp = lax.axis_index("dp")
    y, x, c = dp // 8, lax.rem(dp // 2, 4), lax.rem(dp, 2)

    def zpeer(o):
        return (dp, lax.rem(z + o, NZ))

    def xpeer(d):
        return (y * 8 + lax.rem(x + d, 4) * 2 + c, z)

    def ypeer(d):
        return (lax.rem(y + d, 4) * 8 + x * 2 + c, z)

    sibling = (y * 8 + x * 2 + 1 - c, z)

    def remote(src, dst, ssem, rsem, dev):
        return pltpu.make_async_remote_copy(
            src_ref=src, dst_ref=dst, send_sem=ssem, recv_sem=rsem, device_id=dev, device_id_type=MESH)

    barrier = pltpu.get_barrier_semaphore()
    around = [zpeer(o) for o in GREETED]
    across = [xpeer(d) for d in (1, 2, 3)] + [ypeer(d) for d in (1, 2, 3)] + [sibling]
    for dev in around:
        pl.semaphore_signal(barrier, inc=1, device_id=dev, device_id_type=MESH)

    phon_copy = pltpu.make_async_copy(phon_in.at[0], phon.at[0], in_sem.at[0])
    dur_load = pltpu.make_async_copy(dur_in, dur_row, in_sem.at[1])
    w2_copy = pltpu.make_async_copy(out_w, w2_own, in_sem.at[2])
    gain_copy = pltpu.make_async_copy(gain_in, gain, in_sem.at[3])
    w_copy = pltpu.make_async_copy(conv_w, w, in_sem.at[4])
    for d in (dur_load, phon_copy, w2_copy, w_copy, gain_copy):
        d.start()
    for dev in across:
        pl.semaphore_signal(barrier, inc=1, device_id=dev, device_id_type=MESH)

    dur_all[0] = jnp.zeros((1, 128), jnp.int32)
    dur_load.wait()
    dur_all[0, :, 0:16] = dur_row[...]
    phon_copy.wait()

    def phon_part(o, part):
        if part is None:
            return phon.at[ORDER.index(o)]
        return phon.at[ORDER.index(o), :, pl.ds(512 * part, 512)]

    def w2_part(o, part):
        lanes = pl.ds(128 * ORDER.index(o), 128)
        if part is None:
            return w2.at[y, x, c, :, :, lanes]
        return w2.at[y, x, c, part, :, lanes]

    def dur_part(o, part):
        return dur_all.at[o]

    def gather(place, ssem, rsem, halves=True):
        def copy(held, to, there):
            part = None if there != 8 or not halves else (0 if held < 8 else 1)
            i = 0 if part == 1 else there
            return remote(place(held, part), place(there, part), ssem.at[i], rsem.at[i], zpeer(to))

        direct = {o: [copy(0, o, o)] for o in DIRECT}
        onward = {held: [copy(held, to, there) for to, there in (jobs if halves or held != 10 else jobs[1:])]
                  for held, jobs in ONWARD.items()}
        arrival = dict(direct)
        for held, jobs in ONWARD.items():
            for job, d in zip(jobs[::-1], onward[held][::-1]):
                arrival[job[1]] = arrival.get(job[1], []) + [d]
        return direct, onward, arrival

    pl.semaphore_wait(barrier, len(around) + len(across))

    gathers = [gather(phon_part, ps, pr), gather(dur_part, ds, dr, False), gather(w2_part, ws, wr)]
    rows, durs, cols = [g[2] for g in gathers]

    def arrive(chunks, which):
        for o in which:
            for d in chunks.pop(o, []):
                d.wait_recv()

    for direct, _, _ in gathers[0:2]:
        for o in DIRECT:
            direct[o][0].start()
    w2_copy.wait()
    w2[y, x, c, 0, :, 0:128] = w2_own[0:16]
    w2[y, x, c, 1, :, 0:128] = w2_own[16:32]
    for o in DIRECT:
        gathers[2][0][o][0].start()
    for helds in (DIRECT[0:2], (6, 10)):
        for _, onward, arrival in gathers:
            for held in helds:
                arrive(arrival, (held,))
                for d in onward[held]:
                    d.start()

    def products(begin, end):
        rows = phon[begin:end].reshape(16 * (end - begin), 1024)
        for k in range(0, TAPS, 2):
            taps = [w[t] for t in range(k, min(k + 2, TAPS))]
            cols = jnp.concatenate(taps, axis=1) if len(taps) > 1 else taps[0]
            prod = jnp.dot(rows, cols, preferred_element_type=F32)
            high = prod.astype(BF)
            low = (prod - high.astype(F32)).astype(BF)
            width = 128 * len(taps)
            zc[16 * begin:16 * end, 128 * k:128 * k + width] = high
            zc[256 + 16 * begin:256 + 16 * end, 128 * k:128 * k + width] = low

    def spread(i):
        lanes = pl.ds(128 * WAVES[i][0], 128 * (WAVES[i][1] - WAVES[i][0]))
        first, second, cross = [], [], []
        own = [w2.at[y, x, c, h, :, lanes] for h in (0, 1)]
        row, column = w2.at[y, :, c, 0, :, lanes], w2.at[:, x, c, 1, :, lanes]
        for d in (1, 3, 2):
            first.append(remote(own[0], own[0], xs.at[i, d], xr.at[i, d], xpeer(d)))
            first.append(remote(own[1], own[1], xs.at[i, 3 + d], xr.at[i, 3 + d], ypeer(d)))
            second.append(remote(row, row, xs.at[i, 6 + d], xr.at[i, 6 + d], ypeer(d)))
            second.append(remote(column, column, xs.at[i, 9 + d], xr.at[i, 9 + d], xpeer(d)))
        for d in (0, 1, 3, 2):
            part = w2.at[lax.rem(y + 4 - d, 4), :, c, 0, :, lanes]
            cross.append(remote(part, part, cs.at[i, d], cr.at[i, d], sibling))
            part = w2.at[:, lax.rem(x + 4 - d, 4), c, 1, :, lanes]
            cross.append(remote(part, part, cs.at[i, 4 + d], cr.at[i, 4 + d], sibling))
        return first, second, cross

    spreads = [spread(i) for i in range(len(WAVES))]

    def spread_first(i):
        arrive(cols, ORDER[WAVES[i][0]:WAVES[i][1]])
        for d in spreads[i][0]:
            d.start()

    def spread_second(i):
        first, second, cross = spreads[i]
        for d in first:
            d.wait_recv()
        for d in second + cross[0:2]:
            d.start()

    def spread_cross(i):
        _, second, cross = spreads[i]
        for d, onward in zip(second, cross[2:]):
            d.wait_recv()
            onward.start()

    w_copy.wait()
    for begin, end in GROUPS[0:2]:
        arrive(rows, ORDER[begin:end])
        products(begin, end)
    spread_first(0)

    arrive(durs, range(NZ))
    lengths = jnp.concatenate([dur_all[o] for o in range(NZ)], axis=0).astype(F32).astype(BF)
    begin, end = GROUPS[2]
    col = lax.broadcasted_iota(jnp.int32, (1, 256), 1)
    slot, place = col // 16, lax.rem(col, 16)
    col_off = jnp.zeros_like(col)
    for i, o in enumerate(ORDER):
        col_off = jnp.where(slot == i, o, col_off)
    col_chunk = lax.rem(z + NZ - col_off, NZ)
    row_chunk = lax.rem(z + NZ - lax.broadcasted_iota(jnp.int32, (NZ, 256), 0), NZ)
    lane = lax.broadcasted_iota(jnp.int32, (128, 256), 0)
    upto = ((lane <= place) & (lane < 16)).astype(F32).astype(BF)
    exact = (lane == place).astype(F32).astype(BF)
    whole = (lane < 16).astype(F32).astype(BF)
    within = jnp.dot(lengths, upto, preferred_element_type=F32)
    single = jnp.dot(lengths, exact, preferred_element_type=F32)
    total = jnp.dot(lengths, whole, preferred_element_type=F32)
    same = row_chunk == col_chunk
    ends = jnp.sum(jnp.where(same, within, jnp.where(row_chunk < col_chunk, total, 0.0)), axis=0, keepdims=True)
    sizes = jnp.sum(jnp.where(same, single, 0.0), axis=0, keepdims=True)
    starts = ends - sizes

    def one_hot(first, count):
        frame = (lax.broadcasted_iota(jnp.int32, (count, 256), 0) + first).astype(F32)
        return jnp.where((frame >= starts) & (frame < ends), 1.0, 0.0).astype(BF)

    arrive(rows, ORDER[begin:end])
    products(begin, end)

    def hidden(o):
        block = lax.rem(z + o, NZ)
        pick = one_hot(block * 128 - HALO, ROWS)
        pick = jnp.concatenate([pick, pick], axis=1)
        total = jnp.zeros((128, 128), F32)
        for k in range(0, TAPS, 2):
            width = 128 * min(2, TAPS - k)
            got = jnp.dot(pick, zc[:, 128 * k:128 * k + width], preferred_element_type=F32)
            total = total + got[k:k + 128, 0:128]
            if width > 128:
                total = total + got[k + 1:k + 129, 128:256]
        return jnp.maximum(total, 0.0).astype(BF)

    def hid_copies(o):
        return [remote(hid_out.at[o, pl.ds(64 * k, 64)], hid_in.at[o, pl.ds(64 * k, 64)], hs.at[k, o], hr.at[k, o], zpeer(o))
                for k in (0, 1)]

    def send_hidden(i, carry):
        o = lax.rem(8 + 7 * i, NZ)
        hid_out[o] = hidden(o)
        for d in hid_copies(o):
            d.start()
        return carry

    lax.fori_loop(0, 4, send_hidden, 0)
    spread_first(1)
    lax.fori_loop(4, 8, send_hidden, 0)
    lax.fori_loop(9, NZ, send_hidden, 0)
    spread_second(0)
    spread_second(1)
    hid_in[0] = hidden(0)

    acc[...] = jnp.dot(one_hot(z * 128, 128), phon[...].reshape(256, 1024), preferred_element_type=F32)

    for i in range(len(WAVES)):
        spread_cross(i)
    for _, _, cross in spreads:
        for d in cross:
            d.wait_recv()

    order = [(8 + 7 * i) % NZ for i in range(NZ)]
    groups = (order[0:4], order[4:8], [0] + order[9:12], order[12:14], order[14:16])
    for group in groups:
        for o in group:
            if o:
                for d in hid_copies(o):
                    d.wait_recv()
        left = jnp.concatenate([hid_in[o] for o in group], axis=1)
        slots = [ORDER.index(o) for o in group]
        right = jnp.concatenate(
            [w2[:, :, :, :, :, 128 * i:128 * i + 128].reshape(1024, 128) for i in slots], axis=1)
        acc[...] += lax.dot_general(left, right, (((1,), (1,)), ((), ())), preferred_element_type=F32)

    gain_copy.wait()

    def norm(i, carry):
        rows = pl.ds(pl.multiple_of(i * 16, 16), 16)
        summed = acc[rows, :]
        centered = summed - jnp.mean(summed, axis=-1, keepdims=True)
        spread = jnp.mean(centered * centered, axis=-1, keepdims=True)
        out[0, rows, :] = (centered * lax.rsqrt(spread + 1e-5) * gain[...]).astype(BF)
        return carry

    lax.fori_loop(0, 8, norm, 0, unroll=True)

    for direct, onward, _ in gathers:
        for jobs in [*direct.values(), *onward.values()]:
            for d in jobs:
                d.wait_send()
    for first, second, cross in spreads:
        for d in first + second + cross:
            d.wait_send()
    for o in range(1, NZ):
        for d in hid_copies(o):
            d.wait_send()


def on_device(phonemes, durations, conv_weight, out_weight, norm_gain):
    vmem = pl.BlockSpec(memory_space=pltpu.VMEM)
    sems = pltpu.SemaphoreType.DMA
    return pl.pallas_call(
        kernel,
        out_shape=pltpu.VMEM((1, 128, 1024), BF),
        in_specs=[pl.BlockSpec(memory_space=pltpu.HBM)] * 5,
        out_specs=vmem,
        scratch_shapes=[
            pltpu.VMEM((NZ, 16, 1024), BF),
            pltpu.VMEM((1, 16), jnp.int32),
            pltpu.VMEM((NZ, 1, 128), jnp.int32),
            pltpu.VMEM((TAPS, 1024, 128), BF),
            pltpu.VMEM((32, 128), BF),
            pltpu.VMEM((1, 1024), F32),
            pltpu.VMEM((512, TAPS * 128), BF),
            pltpu.VMEM((4, 4, 2, 2, 16, 2048), BF),
            pltpu.VMEM((NZ, 128, 128), BF),
            pltpu.VMEM((NZ, 128, 128), BF),
            pltpu.VMEM((128, 1024), F32),
            sems((5,)), sems((16,)), sems((16,)), sems((16,)), sems((16,)), sems((16,)), sems((16,)),
            sems((2, 13)), sems((2, 13)), sems((2, 8)), sems((2, 8)), sems((2, 16)), sems((2, 16)),
        ],
        compiler_params=pltpu.CompilerParams(
            collective_id=0, has_side_effects=True, vmem_limit_bytes=63 * 1024 * 1024),
        cost_estimate=pl.CostEstimate(flops=4_000_000_000, bytes_accessed=4_000_000, transcendentals=0),
    )(phonemes, durations, conv_weight, out_weight.T, norm_gain.reshape(1, 1024))


def solution(mesh):
    placed = (P("dp", "tm", None), P("dp", "tm"), P(None, None, "tm"), P("tm", "dp"), P())
    return jax.shard_map(
        on_device, mesh=mesh, in_specs=placed, out_specs=P("dp", "tm", None), check_vma=False
    )
```
